32 devices in a mesh: case: 2 (over x), elem: 16 (over z, y, core).
Axes of the slice: x: 2, y: 2, z: 4, core: 2. Of those that a mesh axis runs over, the one named last changes fastest.
Arguments:
- load_coef: bfloat16 [1024, 512], P(('case', 'elem')), may hold values from -13 to 13
- mantissa: bfloat16 [512, 3, 16384], P(None, None, 'elem'), may hold values from -0.25 to 0.25
- scale_exp: int32 [512, 3, 128], P(None, None, 'elem'), may hold values from -1 to 1
- lin_coef: float32 [2, 16384], P(None, 'elem'), may hold values from -0.5 to 0.5
- quad_coef: float32 [3, 16384], P(None, 'elem'), may hold values from 0.05 to 0.3
- cross_coef: float32 [16384], P('elem'), may hold values from -0.1 to 0.1
- ply_count: int32 [16384], P('elem'), may hold values from 0 to 7
- cotangent: float32 [1024], P('case'), may hold values from -6 to 6
Outputs:
- load_grad: float32 [1024, 512], P(('case', 'elem'))
- coef_grad: float32 [6, 16384], P(None, 'elem')
The draws below stay inside these ranges and needn't reach their ends.
All inputs are finite; a program needn't handle non-finite values.
Results may differ from the reference program's by a relative error of at most 0.0065.
Values may be sent and summed in bfloat16 or wider, within the bound.
No kernel may reach another device: no remote copies, remote signals or barrier semaphores. Data moves between devices by JAX's collectives and lax.ppermute only.
A program may use at most 64 MiB of HBM per device.

```python
import math
import jax
import jax.numpy as jnp
import numpy as np
from jax import lax

U = 512
BLK = 128
CASES = 1024
COLS = 16384
N_ELEM = 16


def draw_load_coef(key, part):
    base = 0.5 * jax.random.normal(key, (CASES, U), jnp.float32)
    return jnp.clip(base, -3.0, 3.0).astype(jnp.bfloat16)


def plant(array, own_key, smallest, largest):
    shape = array.shape
    spot = [jax.random.randint(jax.random.fold_in(own_key, axis), (), 0, shape[axis]) for axis in range(len(shape))]
    array = array.at[tuple(spot)].set(smallest)
    longest = shape.index(max(shape))
    spot[longest] = (spot[longest] + 1) % shape[longest]
    return array.at[tuple(spot)].set(largest)


def steps_of(key, extent, cuts, smallest, high):
    gain = 1.0
    for axis_at, blocks in cuts:
        draws = jax.random.uniform(jax.random.fold_in(jax.random.fold_in(key, 6), axis_at), (blocks,), jnp.float32, smallest / len(cuts), high / len(cuts))
        gain = gain * jnp.repeat(jnp.exp(draws), extent[axis_at] // blocks).reshape((-1,) + (1,) * (len(extent) - 1 - axis_at))
    return gain


def rank_table(number_of, slope):
    weights = [(1 << 20) // math.isqrt(standing ** slope) + 1 for standing in range(1, number_of + 1)]
    deviation = 1 + sum(weights) // (1 << 30)
    return np.cumsum(np.array([max(1, weight // deviation) for weight in weights]))


def skewed_ids(key, dims, number_of, skew):
    grid = rank_table(number_of, skew)
    lot = jax.random.randint(jax.random.fold_in(key, 1), dims, 0, int(grid[number_of - 1]))
    standing = jnp.searchsorted(jnp.asarray(grid, jnp.int32), lot, side="right")
    return jax.random.permutation(jax.random.fold_in(key, 2), number_of)[standing].astype(jnp.int32)


def gaussian(rng, dims, deviation, bound, cuts=(), kind=jnp.bfloat16):
    result = deviation * jax.random.normal(rng, dims, jnp.float32)
    if cuts:
        result = result * steps_of(rng, dims, cuts, -0.22, 0.18)
    return jnp.clip(result, -bound, bound).astype(kind)


def setup_inputs(seed: int = 0) -> dict:
    seeds = jax.random.split(jax.random.key(seed), 9)
    return {
        "load_coef": draw_load_coef(jax.random.fold_in(seeds[8], 71), 0),
        "mantissa": gaussian(seeds[1], (U, 3, COLS), U ** -0.5, 0.25, ((2, 16),)),
        "scale_exp": plant(jax.random.randint(seeds[2], (U, 3, COLS // BLK), -1, 2), jax.random.fold_in(seeds[2], 1), -1, 1).astype(jnp.int32),
        "lin_coef": jnp.clip(jax.random.uniform(seeds[3], (2, COLS), jnp.float32, -0.5, 0.5) * steps_of(seeds[3], (2, COLS), ((1, 16),), -0.4, 0.0), -0.5, 0.5),
        "quad_coef": jnp.clip(jnp.exp(math.log(0.3) - 1.7917595 * jax.random.uniform(seeds[4], (3, COLS), jnp.float32) ** steps_of(seeds[4], (3, COLS), ((1, 16),), -0.2, 0.2)), 0.05, 0.3),
        "cross_coef": jnp.clip(jax.random.uniform(seeds[5], (COLS,), jnp.float32, -0.1, 0.1) * steps_of(seeds[5], (COLS,), ((0, 16),), -0.4, 0.0), -0.1, 0.1),
        "ply_count": plant(skewed_ids(seeds[6], (COLS,), 8, 2), jax.random.fold_in(seeds[6], 3), 0, 7).astype(jnp.int32),
        "cotangent": gaussian(seeds[7], (CASES,), 1.0, 6.0, ((0, 2),), jnp.float32),
    }


rho_value = 1.0


def dequant(mant, expo):
    units, comps, width = mant.shape
    blocks = expo.shape[-1]
    factor = jnp.exp2(expo.astype(jnp.float32)).astype(jnp.bfloat16)
    scaled = mant.reshape(units, comps, blocks, width // blocks) * factor[..., None]
    return scaled.reshape(units, comps * width)


def tsai_wu(first, second, shear, lin, quad, cross):
    return (lin[0] * first + lin[1] * second + quad[0] * first * first
            + quad[1] * second * second + quad[2] * shear * shear
            + 2.0 * cross * first * second)


def reference(load_coef, mantissa, scale_exp, lin_coef, quad_coef, cross_coef, ply_count, cotangent):
    nblk = N_ELEM
    width = mantissa.shape[2] // nblk
    mant_blocks = mantissa.reshape(U, 3, nblk, width).transpose(2, 0, 1, 3)
    exp_blocks = scale_exp.reshape(U, 3, nblk, -1).transpose(2, 0, 1, 3)
    lin_blocks = lin_coef.reshape(2, nblk, width).transpose(1, 0, 2)
    quad_blocks = quad_coef.reshape(3, nblk, width).transpose(1, 0, 2)
    cross_blocks = cross_coef.reshape(nblk, width)
    ply_blocks = (ply_count + 1).astype(jnp.float32).reshape(nblk, width)

    def forward(pieces):
        mant, expo = pieces
        fields = dequant(mant, expo)
        return jnp.dot(load_coef, fields, preferred_element_type=jnp.float32).reshape(-1, 3, width)

    stress = lax.map(forward, (mant_blocks, exp_blocks))
    index = tsai_wu(stress[:, :, 0], stress[:, :, 1], stress[:, :, 2],
                    lin_blocks.transpose(1, 0, 2)[:, :, None, :],
                    quad_blocks.transpose(1, 0, 2)[:, :, None, :],
                    cross_blocks[:, None, :])
    peak = jnp.max(index, axis=(0, 2))
    total = jnp.sum(ply_blocks[:, None, :] * jnp.exp(rho_value * (index - peak[None, :, None])), axis=(0, 2))
    envelope = peak + jnp.log(total) / rho_value

    def backward(carry, pieces):
        mant, expo, block_stress, block_index, lin, quad, cross, plies = pieces
        fields = dequant(mant, expo)
        first = block_stress[:, 0]
        second = block_stress[:, 1]
        shear = block_stress[:, 2]
        weight = cotangent[:, None] * plies[None, :] * jnp.exp(rho_value * (block_index - envelope[:, None]))
        grad_one = weight * (lin[0] + 2.0 * quad[0] * first + 2.0 * cross * second)
        grad_two = weight * (lin[1] + 2.0 * quad[1] * second + 2.0 * cross * first)
        grad_three = weight * (2.0 * quad[2] * shear)
        dstress = jnp.concatenate([grad_one, grad_two, grad_three], axis=1).astype(jnp.bfloat16)
        carry = carry + lax.dot_general(dstress, fields, (((1,), (1,)), ((), ())),
                                        preferred_element_type=jnp.float32)
        coefs = jnp.stack([jnp.sum(weight * first, axis=0), jnp.sum(weight * second, axis=0),
                           jnp.sum(weight * first * first, axis=0), jnp.sum(weight * second * second, axis=0),
                           jnp.sum(weight * shear * shear, axis=0), jnp.sum(weight * 2.0 * first * second, axis=0)])
        return carry, coefs

    start = jnp.zeros((load_coef.shape[0], U), jnp.float32)
    load_grad, coefs = lax.scan(backward, start, (mant_blocks, exp_blocks, stress, index,
                                                  lin_blocks, quad_blocks, cross_blocks, ply_blocks))
    coef_grad = coefs.transpose(1, 0, 2).reshape(6, -1)
    return load_grad, coef_grad
```

```python
import functools

import jax
import jax.numpy as jnp
from jax import lax
from jax.experimental import pallas as pl
from jax.experimental.pallas import tpu as pltpu
from jax.sharding import PartitionSpec as P

JB = 256
VMEM = pltpu.VMEM


def vmem_call(kernel, out_shape, scratch_shapes=(), flops=0, nbytes=0, exps=0, n_in=0, smem=(), limit=40):
    return pl.pallas_call(
        kernel,
        out_shape=out_shape,
        in_specs=[
            pl.BlockSpec(memory_space=pltpu.SMEM if i in smem else VMEM) for i in range(n_in)
        ],
        out_specs=jax.tree.map(lambda _: pl.BlockSpec(memory_space=VMEM), out_shape),
        scratch_shapes=list(scratch_shapes),
        cost_estimate=pl.CostEstimate(flops=flops, bytes_accessed=nbytes, transcendentals=exps),
        compiler_params=pltpu.CompilerParams(vmem_limit_bytes=limit << 20),
    )


def to_lanes(column, rows):
    step = min(rows, 128)
    parts = []
    for at in range(0, rows, step):
        square = jnp.broadcast_to(column[at : at + step], (step, 128))
        parts.append(jnp.transpose(square)[0:1, :])
    return jnp.concatenate(parts, axis=1)


def to_rows(row, at):
    return jnp.transpose(jnp.broadcast_to(row[:, at : at + 128], (128, 128)))


def prep_kernel(mant_ref, exp_ref, out_ref):
    comps, units, width = mant_ref.shape
    blocks = exp_ref.shape[1]
    span = width // blocks
    factor = jnp.exp2(exp_ref[...].astype(jnp.float32)).reshape(comps * blocks, units)
    pad = jnp.zeros((128 - comps * blocks, units), jnp.float32)
    columns = jnp.transpose(jnp.concatenate([factor, pad], axis=0))
    for k in range(comps):
        for b in range(blocks):
            gain = jnp.broadcast_to(columns[:, k * blocks + b : k * blocks + b + 1], (units, span))
            value = mant_ref[k, :, b * span : (b + 1) * span] * gain.astype(jnp.bfloat16)
            first = b * span
            at = (first // JB) * (comps * JB) + k * JB + first % JB
            out_ref[:, at : at + span] = value


def main_kernel(n, a_ref, f_ref, lin_ref, quad_ref, cross_ref, ply_ref, *refs):
    own_ref = refs[0]
    send_refs = refs[1:n]
    stat_ref, s_ref, w_ref, idx, d, acc = refs[n:]
    cases = a_ref.shape[0]
    width = lin_ref.shape[1]
    rows = cases // n
    tile = 32
    peak = jnp.full((cases, 128), -jnp.inf, jnp.float32)
    for jb in range(width // JB):
        cols = slice(jb * JB, (jb + 1) * JB)
        base = jb * 3 * JB
        s_ref[:, base : base + 3 * JB] = jnp.dot(
            a_ref[...], f_ref[:, base : base + 3 * JB], preferred_element_type=jnp.float32
        )
        f1, f2 = lin_ref[0:1, cols], lin_ref[1:2, cols]
        f11, f22, f66 = quad_ref[0:1, cols], quad_ref[1:2, cols], quad_ref[2:3, cols]
        f12 = 2.0 * cross_ref[0:1, cols]
        tops = []
        for at in range(0, cases, tile):
            r = slice(at, at + tile)
            s1 = s_ref[r, base : base + JB]
            s2 = s_ref[r, base + JB : base + 2 * JB]
            t = s_ref[r, base + 2 * JB : base + 3 * JB]
            index = s1 * (f1 + f11 * s1 + f12 * s2) + s2 * (f2 + f22 * s2) + f66 * (t * t)
            idx[r, cols] = index
            top = index[:, 0:128]
            for c in range(128, JB, 128):
                top = jnp.maximum(top, index[:, c : c + 128])
            tops.append(top)
        peak = jnp.maximum(peak, jnp.concatenate(tops, axis=0))
    peak = jnp.max(peak, axis=1, keepdims=True)

    total = jnp.zeros((cases, 128), jnp.float32)
    for jb in range(width // JB):
        cols = slice(jb * JB, (jb + 1) * JB)
        base = jb * 3 * JB
        f1, f2 = lin_ref[0:1, cols], lin_ref[1:2, cols]
        q11, q22, q66 = 2.0 * quad_ref[0:1, cols], 2.0 * quad_ref[1:2, cols], 2.0 * quad_ref[2:3, cols]
        f12 = 2.0 * cross_ref[0:1, cols]
        plies = (ply_ref[0:1, cols] + 1).astype(jnp.float32)
        sums = []
        for at in range(0, cases, tile):
            r = slice(at, at + tile)
            s1 = s_ref[r, base : base + JB]
            s2 = s_ref[r, base + JB : base + 2 * JB]
            t = s_ref[r, base + 2 * JB : base + 3 * JB]
            w = plies * jnp.exp(idx[r, cols] - peak[r])
            w_ref[r, cols] = w
            part = w[:, 0:128]
            for c in range(128, JB, 128):
                part = part + w[:, c : c + 128]
            sums.append(part)
            d[r, base : base + JB] = (w * (f1 + q11 * s1 + f12 * s2)).astype(jnp.bfloat16)
            d[r, base + JB : base + 2 * JB] = (w * (f2 + q22 * s2 + f12 * s1)).astype(jnp.bfloat16)
            d[r, base + 2 * JB : base + 3 * JB] = (w * (q66 * t)).astype(jnp.bfloat16)
        total = total + jnp.concatenate(sums, axis=0)
        part = lax.dot_general(
            d[:, base : base + 3 * JB],
            f_ref[:, base : base + 3 * JB],
            (((1,), (1,)), ((), ())),
            preferred_element_type=jnp.float32,
        )
        if jb == 0:
            acc[...] = part
        else:
            acc[...] += part
    total = jnp.sum(total, axis=1, keepdims=True)
    stat_ref[0:1, :] = to_lanes(peak, cases)
    stat_ref[1:2, :] = to_lanes(total, cases)
    own_ref[...] = acc[0:rows, :]
    for p in range(1, n):
        send_refs[p - 1][...] = acc[p * rows : (p + 1) * rows, :].astype(jnp.bfloat16)


def swap_lanes(x, which, rows, n):
    lane = lax.broadcasted_iota(jnp.int32, x.shape, 1)
    bit = 1
    while bit < n:
        step = bit * rows
        ahead = jnp.concatenate([x[:, step:], x[:, :step]], axis=1)
        behind = jnp.concatenate([x[:, -step:], x[:, :-step]], axis=1)
        other = jnp.where((lane & step) != 0, behind, ahead)
        x = jnp.where((which & bit) != 0, other, x)
        bit *= 2
    return x


def coef_kernel(n, me_ref, cot_ref, s_ref, w_ref, *refs):
    stat_refs = refs[:n]
    coef_ref, gain_ref, peaks, totals = refs[n:]
    cases = cot_ref.shape[1]
    width = w_ref.shape[1]
    rows = cases // n
    for p in range(n):
        peaks[p : p + 1, :] = stat_refs[p][0:1, :]
        totals[p : p + 1, :] = stat_refs[p][1:2, :]
    which = lax.broadcasted_iota(jnp.int32, (n, cases), 0)
    peak_all = swap_lanes(peaks[...], which, rows, n)
    total_all = swap_lanes(totals[...], which, rows, n)
    mine = jnp.full((8, cases), me_ref[0], jnp.int32)
    cot = swap_lanes(jnp.broadcast_to(cot_ref[...], (8, cases)), mine, rows, n)[0:1]
    peak = jnp.max(peak_all, axis=0, keepdims=True)
    total = jnp.sum(total_all * jnp.exp(peak_all - peak), axis=0, keepdims=True)
    envelope = peak + jnp.log(total)
    gain = cot * jnp.exp(peak_all - envelope)
    square = gain[:, 0:128]
    if n < 128:
        square = jnp.concatenate([square, jnp.zeros((128 - n, 128), jnp.float32)], axis=0)
    gain_ref[...] = jnp.transpose(square)[0:rows]
    mine = gain[0:1]
    scales = [to_rows(mine, at) for at in range(0, cases, 128)]
    for jb in range(width // JB):
        base = jb * 3 * JB
        for c in range(0, JB, 128):
            sums = [jnp.zeros((8, 128), jnp.float32) for _ in range(6)]
            for at in range(0, cases, 8):
                r = slice(at, at + 8)
                s1 = s_ref[r, base + c : base + c + 128]
                s2 = s_ref[r, base + JB + c : base + JB + c + 128]
                t = s_ref[r, base + 2 * JB + c : base + 2 * JB + c + 128]
                local = at % 128
                w = w_ref[r, jb * JB + c : jb * JB + c + 128] * scales[at // 128][local : local + 8]
                a, b = w * s1, w * s2
                for i, v in enumerate((a, b, a * s1, b * s2, w * t * t, a * s2)):
                    sums[i] = sums[i] + v
            for i in range(6):
                line = jnp.sum(sums[i], axis=0, keepdims=True)
                if i == 5:
                    line = 2.0 * line
                coef_ref[i : i + 1, jb * JB + c : jb * JB + c + 128] = line


def combine_kernel(n, gain_ref, own_ref, *refs):
    out_ref = refs[-1]
    value = own_ref[...] * gain_ref[:, 0:1]
    for p in range(1, n):
        value = value + refs[p - 1][...].astype(jnp.float32) * gain_ref[:, p : p + 1]
    out_ref[...] = value


def per_device(n, n_case, load_coef, mantissa, scale_exp, lin_coef, quad_coef, cross_coef, ply_count, cotangent):
    units, comps, width = mantissa.shape
    rows = load_coef.shape[0]
    cases = rows * n
    f32, bf16 = jnp.float32, jnp.bfloat16
    shape = jax.ShapeDtypeStruct

    def swap(x, axis, size, p):
        return lax.ppermute(x, axis, [(i, i ^ p) for i in range(size)])

    gathered = load_coef
    bit = n // 2
    order = [0]
    while bit:
        gathered = jnp.concatenate([gathered, swap(gathered, "elem", n, bit)], axis=0)
        order = order + [p ^ bit for p in order]
        bit //= 2
    place = {p: i for i, p in enumerate(order)}
    gathered = jnp.concatenate(
        [lax.slice_in_dim(gathered, place[p] * rows, place[p] * rows + rows) for p in range(n)]
    )

    fields = vmem_call(
        prep_kernel,
        shape((units, comps * width), bf16),
        flops=units * comps * width,
        nbytes=4 * units * comps * width,
        n_in=2,
    )(jnp.transpose(mantissa, (1, 0, 2)), jnp.transpose(scale_exp, (1, 2, 0)))

    outs = vmem_call(
        functools.partial(main_kernel, n),
        [shape((rows, units), f32)]
        + [shape((rows, units), bf16)] * (n - 1)
        + [shape((2, cases), f32), shape((cases, comps * width), f32), shape((cases, width), f32)],
        scratch_shapes=[
            VMEM((cases, width), f32),
            VMEM((cases, comps * width), bf16),
            VMEM((cases, units), f32),
        ],
        flops=4 * cases * units * comps * width,
        nbytes=2 * units * comps * width + 4 * cases * 4 * width,
        exps=cases * width,
        n_in=6,
    )(gathered, fields, lin_coef, quad_coef, cross_coef.reshape(1, width), ply_count.reshape(1, width))
    own, sends, stat, stress, weight = outs[0], outs[1:n], outs[n], outs[n + 1], outs[n + 2]

    stats = [stat] + [swap(stat, "elem", n, p) for p in range(1, n)]
    parts = [swap(sends[p - 1], "elem", n, p) for p in range(1, n)]

    me = lax.axis_index("elem").astype(jnp.int32).reshape(1)
    coef, gain = vmem_call(
        functools.partial(coef_kernel, n),
        [shape((6, width), f32), shape((rows, 128), f32)],
        scratch_shapes=[VMEM((n, cases), f32), VMEM((n, cases), f32)],
        flops=14 * cases * width,
        nbytes=16 * cases * width,
        n_in=4 + n,
        smem=(0,),
    )(me, cotangent.reshape(1, cases), stress, weight, *stats)
    bit = 1
    while bit < n_case:
        coef = coef + swap(coef, "case", n_case, bit)
        bit *= 2

    load_grad = vmem_call(
        functools.partial(combine_kernel, n),
        shape((rows, units), f32),
        flops=2 * n * rows * units,
        nbytes=2 * n * rows * units,
        n_in=1 + n,
    )(gain, own, *parts)
    return (load_grad, coef)


def solution(mesh):
    n, n_case = mesh.shape["elem"], mesh.shape["case"]
    return jax.shard_map(
        functools.partial(per_device, n, n_case),
        mesh=mesh,
        in_specs=(
            P(("case", "elem"), None),
            P(None, None, "elem"),
            P(None, None, "elem"),
            P(None, "elem"),
            P(None, "elem"),
            P("elem"),
            P("elem"),
            P("case"),
        ),
        out_specs=(P(("case", "elem"), None), P(None, "elem")),
        check_vma=False,
    )
```

```python
import functools

import jax
import jax.numpy as jnp
from jax import lax
from jax.experimental import pallas as pl
from jax.experimental.pallas import tpu as pltpu
from jax.sharding import PartitionSpec as P

JB = 256
VMEM = pltpu.VMEM


def vmem_call(kernel, out_shape, scratch_shapes=(), flops=0, nbytes=0, exps=0, n_in=0, smem=(), limit=40):
    return pl.pallas_call(
        kernel,
        out_shape=out_shape,
        in_specs=[
            pl.BlockSpec(memory_space=pltpu.SMEM if i in smem else VMEM) for i in range(n_in)
        ],
        out_specs=jax.tree.map(lambda _: pl.BlockSpec(memory_space=VMEM), out_shape),
        scratch_shapes=list(scratch_shapes),
        cost_estimate=pl.CostEstimate(flops=flops, bytes_accessed=nbytes, transcendentals=exps),
        compiler_params=pltpu.CompilerParams(vmem_limit_bytes=limit << 20),
    )


def to_lanes(column, rows):
    step = min(rows, 128)
    parts = []
    for at in range(0, rows, step):
        square = jnp.broadcast_to(column[at : at + step], (step, 128))
        parts.append(jnp.transpose(square)[0:1, :])
    return jnp.concatenate(parts, axis=1)


def to_rows(row, at):
    return jnp.transpose(jnp.broadcast_to(row[:, at : at + 128], (128, 128)))


def prep_kernel(mant_ref, exp_ref, out_ref):
    comps, units, width = mant_ref.shape
    blocks = exp_ref.shape[1]
    span = width // blocks
    factor = jnp.exp2(exp_ref[...].astype(jnp.float32)).reshape(comps * blocks, units)
    pad = jnp.zeros((128 - comps * blocks, units), jnp.float32)
    columns = jnp.transpose(jnp.concatenate([factor, pad], axis=0))
    for k in range(comps):
        for b in range(blocks):
            gain = jnp.broadcast_to(columns[:, k * blocks + b : k * blocks + b + 1], (units, span))
            value = mant_ref[k, :, b * span : (b + 1) * span] * gain.astype(jnp.bfloat16)
            first = b * span
            at = (first // JB) * (comps * JB) + k * JB + first % JB
            out_ref[:, at : at + span] = value


def main_kernel(n, a_ref, f_ref, lin_ref, quad_ref, cross_ref, ply_ref, part_ref, stat_ref, s_ref, w_ref, idx, d, acc):
    cases = a_ref.shape[0]
    width = lin_ref.shape[1]
    tile = 32
    peak = jnp.full((cases, 128), -jnp.inf, jnp.float32)
    for jb in range(width // JB):
        cols = slice(jb * JB, (jb + 1) * JB)
        base = jb * 3 * JB
        s_ref[:, base : base + 3 * JB] = jnp.dot(
            a_ref[...], f_ref[:, base : base + 3 * JB], preferred_element_type=jnp.float32
        )
        f1, f2 = lin_ref[0:1, cols], lin_ref[1:2, cols]
        f11, f22, f66 = quad_ref[0:1, cols], quad_ref[1:2, cols], quad_ref[2:3, cols]
        f12 = 2.0 * cross_ref[0:1, cols]
        tops = []
        for at in range(0, cases, tile):
            r = slice(at, at + tile)
            s1 = s_ref[r, base : base + JB]
            s2 = s_ref[r, base + JB : base + 2 * JB]
            t = s_ref[r, base + 2 * JB : base + 3 * JB]
            index = s1 * (f1 + f11 * s1 + f12 * s2) + s2 * (f2 + f22 * s2) + f66 * (t * t)
            idx[r, cols] = index
            top = index[:, 0:128]
            for c in range(128, JB, 128):
                top = jnp.maximum(top, index[:, c : c + 128])
            tops.append(top)
        peak = jnp.maximum(peak, jnp.concatenate(tops, axis=0))
    peak = jnp.max(peak, axis=1, keepdims=True)

    total = jnp.zeros((cases, 128), jnp.float32)
    for jb in range(width // JB):
        cols = slice(jb * JB, (jb + 1) * JB)
        base = jb * 3 * JB
        f1, f2 = lin_ref[0:1, cols], lin_ref[1:2, cols]
        q11, q22, q66 = 2.0 * quad_ref[0:1, cols], 2.0 * quad_ref[1:2, cols], 2.0 * quad_ref[2:3, cols]
        f12 = 2.0 * cross_ref[0:1, cols]
        plies = (ply_ref[0:1, cols] + 1).astype(jnp.float32)
        sums = []
        for at in range(0, cases, tile):
            r = slice(at, at + tile)
            s1 = s_ref[r, base : base + JB]
            s2 = s_ref[r, base + JB : base + 2 * JB]
            t = s_ref[r, base + 2 * JB : base + 3 * JB]
            w = plies * jnp.exp(idx[r, cols] - peak[r])
            w_ref[r, cols] = w
            part = w[:, 0:128]
            for c in range(128, JB, 128):
                part = part + w[:, c : c + 128]
            sums.append(part)
            d[r, base : base + JB] = (w * (f1 + q11 * s1 + f12 * s2)).astype(jnp.bfloat16)
            d[r, base + JB : base + 2 * JB] = (w * (f2 + q22 * s2 + f12 * s1)).astype(jnp.bfloat16)
            d[r, base + 2 * JB : base + 3 * JB] = (w * (q66 * t)).astype(jnp.bfloat16)
        total = total + jnp.concatenate(sums, axis=0)
        part = lax.dot_general(
            d[:, base : base + 3 * JB],
            f_ref[:, base : base + 3 * JB],
            (((1,), (1,)), ((), ())),
            preferred_element_type=jnp.float32,
        )
        if jb == 0:
            acc[...] = part
        elif jb < width // JB - 1:
            acc[...] += part
        else:
            part_ref[...] = (acc[...] + part).astype(jnp.bfloat16)
    total = jnp.sum(total, axis=1, keepdims=True)
    both = jnp.concatenate([to_lanes(peak, cases), to_lanes(total, cases)], axis=0)
    for s in range(n):
        stat_ref[s] = both


def coef_kernel(n, me_ref, cot_ref, s_ref, w_ref, stat_ref, coef_ref, gain_ref, peaks, totals, turned):
    cases = cot_ref.shape[1]
    width = w_ref.shape[1]
    rows = cases // n
    for p in range(n):
        peaks[p : p + 1, :] = stat_ref[p, 0:1, :]
        totals[p : p + 1, :] = stat_ref[p, 1:2, :]
    peak_all = peaks[...]
    peak = jnp.max(peak_all, axis=0, keepdims=True)
    total = jnp.sum(totals[...] * jnp.exp(peak_all - peak), axis=0, keepdims=True)
    envelope = peak + jnp.log(total)
    gain = cot_ref[...] * jnp.exp(peak_all - envelope)
    peaks[...] = gain
    for at in range(0, cases, 128):
        square = gain[:, at : at + 128]
        if n < 128:
            square = jnp.concatenate([square, jnp.zeros((128 - n, 128), jnp.float32)], axis=0)
        turned[at : at + 128, :] = jnp.transpose(square)
    me = me_ref[0]
    gain_ref[...] = turned[pl.ds(pl.multiple_of(me * rows, rows), rows), :]
    mine = peaks[pl.ds(me, 1), :]
    scales = [to_rows(mine, at) for at in range(0, cases, 128)]
    for jb in range(width // JB):
        base = jb * 3 * JB
        for c in range(0, JB, 128):
            sums = [jnp.zeros((8, 128), jnp.float32) for _ in range(6)]
            for at in range(0, cases, 8):
                r = slice(at, at + 8)
                s1 = s_ref[r, base + c : base + c + 128]
                s2 = s_ref[r, base + JB + c : base + JB + c + 128]
                t = s_ref[r, base + 2 * JB + c : base + 2 * JB + c + 128]
                local = at % 128
                w = w_ref[r, jb * JB + c : jb * JB + c + 128] * scales[at // 128][local : local + 8]
                a, b = w * s1, w * s2
                for i, v in enumerate((a, b, a * s1, b * s2, w * t * t, a * s2)):
                    sums[i] = sums[i] + v
            for i in range(6):
                line = jnp.sum(sums[i], axis=0, keepdims=True)
                if i == 5:
                    line = 2.0 * line
                coef_ref[i : i + 1, jb * JB + c : jb * JB + c + 128] = line


def combine_kernel(n, gain_ref, part_ref, out_ref):
    rows = out_ref.shape[0]
    value = part_ref[0].astype(jnp.float32) * gain_ref[:, 0:1]
    for p in range(1, n):
        value = value + part_ref[p].astype(jnp.float32) * gain_ref[:, p : p + 1]
    out_ref[...] = value


def per_device(n, n_case, load_coef, mantissa, scale_exp, lin_coef, quad_coef, cross_coef, ply_count, cotangent):
    units, comps, width = mantissa.shape
    rows = load_coef.shape[0]
    cases = rows * n
    f32, bf16 = jnp.float32, jnp.bfloat16
    shape = jax.ShapeDtypeStruct

    copies = jnp.broadcast_to(load_coef[None], (n, rows, units))
    gathered = lax.all_to_all(copies, "elem", 0, 0).reshape(cases, units)

    fields = vmem_call(
        prep_kernel,
        shape((units, comps * width), bf16),
        flops=units * comps * width,
        nbytes=4 * units * comps * width,
        n_in=2,
    )(jnp.transpose(mantissa, (1, 0, 2)), jnp.transpose(scale_exp, (1, 2, 0)))

    part, stat, stress, weight = vmem_call(
        functools.partial(main_kernel, n),
        [
            shape((cases, units), bf16),
            shape((n, 2, cases), f32),
            shape((cases, comps * width), f32),
            shape((cases, width), f32),
        ],
        scratch_shapes=[
            VMEM((cases, width), f32),
            VMEM((cases, comps * width), bf16),
            VMEM((cases, units), f32),
        ],
        flops=4 * cases * units * comps * width,
        nbytes=2 * units * comps * width + 4 * cases * 4 * width,
        exps=cases * width,
        n_in=6,
    )(gathered, fields, lin_coef, quad_coef, cross_coef.reshape(1, width), ply_count.reshape(1, width))

    stats = lax.all_to_all(stat, "elem", 0, 0)
    parts = lax.all_to_all(part.reshape(n, rows, units), "elem", 0, 0)

    me = lax.axis_index("elem").astype(jnp.int32).reshape(1)
    coef, gain = vmem_call(
        functools.partial(coef_kernel, n),
        [shape((6, width), f32), shape((rows, 128), f32)],
        scratch_shapes=[VMEM((n, cases), f32), VMEM((n, cases), f32), VMEM((cases, 128), f32)],
        flops=14 * cases * width,
        nbytes=16 * cases * width,
        n_in=5,
        smem=(0,),
    )(me, cotangent.reshape(1, cases), stress, weight, stats)
    bit = 1
    while bit < n_case:
        coef = coef + lax.ppermute(coef, "case", [(i, i ^ bit) for i in range(n_case)])
        bit *= 2

    load_grad = vmem_call(
        functools.partial(combine_kernel, n),
        shape((rows, units), f32),
        flops=2 * n * rows * units,
        nbytes=2 * n * rows * units,
        n_in=2,
    )(gain, parts)
    return (load_grad, coef)


def solution(mesh):
    n, n_case = mesh.shape["elem"], mesh.shape["case"]
    return jax.shard_map(
        functools.partial(per_device, n, n_case),
        mesh=mesh,
        in_specs=(
            P(("case", "elem"), None),
            P(None, None, "elem"),
            P(None, None, "elem"),
            P(None, "elem"),
            P(None, "elem"),
            P("elem"),
            P("elem"),
            P("case"),
        ),
        out_specs=(P(("case", "elem"), None), P(None, "elem")),
        check_vma=False,
    )
```

```python
import functools

import jax
import jax.numpy as jnp
from jax import lax
from jax.experimental import pallas as pl
from jax.experimental.pallas import tpu as pltpu
from jax.sharding import PartitionSpec as P

JB = 256
VMEM = pltpu.VMEM


def vmem_call(kernel, out_shape, scratch_shapes=(), flops=0, nbytes=0, exps=0, n_in=0, smem=(), limit=16):
    return pl.pallas_call(
        kernel,
        out_shape=out_shape,
        in_specs=[
            pl.BlockSpec(memory_space=pltpu.SMEM if i in smem else VMEM) for i in range(n_in)
        ],
        out_specs=jax.tree.map(lambda _: pl.BlockSpec(memory_space=VMEM), out_shape),
        scratch_shapes=list(scratch_shapes),
        cost_estimate=pl.CostEstimate(flops=flops, bytes_accessed=nbytes, transcendentals=exps),
        compiler_params=pltpu.CompilerParams(vmem_limit_bytes=limit << 20),
    )


def to_lanes(column, rows):
    step = min(rows, 128)
    parts = []
    for at in range(0, rows, step):
        square = jnp.broadcast_to(column[at : at + step], (step, 128))
        parts.append(jnp.transpose(square)[0:1, :])
    return jnp.concatenate(parts, axis=1)


def to_rows(row, at):
    return jnp.transpose(jnp.broadcast_to(row[:, at : at + 128], (128, 128)))


def prep_kernel(mant_ref, exp_ref, cot_ref, out_ref, cot_out_ref):
    cot_out_ref[...] = cot_ref[...]
    comps, units, width = mant_ref.shape
    blocks = exp_ref.shape[1]
    span = width // blocks
    factor = jnp.exp2(exp_ref[...].astype(jnp.float32)).reshape(comps * blocks, units)
    pad = jnp.zeros((128 - comps * blocks, units), jnp.float32)
    columns = jnp.transpose(jnp.concatenate([factor, pad], axis=0))
    for k in range(comps):
        for b in range(blocks):
            gain = jnp.broadcast_to(columns[:, k * blocks + b : k * blocks + b + 1], (units, span))
            value = mant_ref[k, :, b * span : (b + 1) * span] * gain.astype(jnp.bfloat16)
            first = b * span
            at = (first // JB) * (comps * JB) + k * JB + first % JB
            out_ref[:, at : at + span] = value


def main_kernel(mine_ref, other_ref, f_ref, lin_ref, quad_ref, cross_ref, ply_ref, keep_ref, send_ref, stat_ref, s_ref, w_ref, idx, d, acc):
    half = mine_ref.shape[0]
    cases = 2 * half
    width = lin_ref.shape[1]
    tile = 32
    peak = jnp.full((cases, 128), -jnp.inf, jnp.float32)
    for jb in range(width // JB):
        cols = slice(jb * JB, (jb + 1) * JB)
        base = jb * 3 * JB
        a = jnp.concatenate([mine_ref[...], other_ref[...]], axis=0)
        s_ref[:, base : base + 3 * JB] = jnp.dot(
            a, f_ref[:, base : base + 3 * JB], preferred_element_type=jnp.float32
        )
        f1, f2 = lin_ref[0:1, cols], lin_ref[1:2, cols]
        f11, f22, f66 = quad_ref[0:1, cols], quad_ref[1:2, cols], quad_ref[2:3, cols]
        f12 = 2.0 * cross_ref[0:1, cols]
        tops = []
        for at in range(0, cases, tile):
            r = slice(at, at + tile)
            s1 = s_ref[r, base : base + JB]
            s2 = s_ref[r, base + JB : base + 2 * JB]
            t = s_ref[r, base + 2 * JB : base + 3 * JB]
            index = s1 * (f1 + f11 * s1 + f12 * s2) + s2 * (f2 + f22 * s2) + f66 * (t * t)
            idx[r, cols] = index
            top = index[:, 0:128]
            for c in range(128, JB, 128):
                top = jnp.maximum(top, index[:, c : c + 128])
            tops.append(top)
        peak = jnp.maximum(peak, jnp.concatenate(tops, axis=0))
    peak = jnp.max(peak, axis=1, keepdims=True)

    total = jnp.zeros((cases, 128), jnp.float32)
    for jb in range(width // JB):
        cols = slice(jb * JB, (jb + 1) * JB)
        base = jb * 3 * JB
        f1, f2 = lin_ref[0:1, cols], lin_ref[1:2, cols]
        q11, q22, q66 = 2.0 * quad_ref[0:1, cols], 2.0 * quad_ref[1:2, cols], 2.0 * quad_ref[2:3, cols]
        f12 = 2.0 * cross_ref[0:1, cols]
        plies = (ply_ref[0:1, cols] + 1).astype(jnp.float32)
        sums = []
        for at in range(0, cases, tile):
            r = slice(at, at + tile)
            s1 = s_ref[r, base : base + JB]
            s2 = s_ref[r, base + JB : base + 2 * JB]
            t = s_ref[r, base + 2 * JB : base + 3 * JB]
            w = plies * jnp.exp(idx[r, cols] - peak[r])
            w_ref[r, cols] = w
            part = w[:, 0:128]
            for c in range(128, JB, 128):
                part = part + w[:, c : c + 128]
            sums.append(part)
            d[r, base : base + JB] = (w * (f1 + q11 * s1 + f12 * s2)).astype(jnp.bfloat16)
            d[r, base + JB : base + 2 * JB] = (w * (f2 + q22 * s2 + f12 * s1)).astype(jnp.bfloat16)
            d[r, base + 2 * JB : base + 3 * JB] = (w * (q66 * t)).astype(jnp.bfloat16)
        total = total + jnp.concatenate(sums, axis=0)
        part = lax.dot_general(
            d[:, base : base + 3 * JB],
            f_ref[:, base : base + 3 * JB],
            (((1,), (1,)), ((), ())),
            preferred_element_type=jnp.float32,
        )
        if jb == 0:
            acc[...] = part
        elif jb < width // JB - 1:
            acc[...] += part
        else:
            keep_ref[...] = acc[0:half] + part[0:half]
            send_ref[...] = (acc[half:] + part[half:]).astype(jnp.bfloat16)
    total = jnp.sum(total, axis=1, keepdims=True)
    stat_ref[0:1, :] = to_lanes(peak, cases)
    stat_ref[1:2, :] = to_lanes(total, cases)


def swap_halves(x):
    half = x.shape[1] // 2
    return jnp.concatenate([x[:, half:], x[:, :half]], axis=1)


def merge_kernel(chips, keep_ref, got_ref, stat_ref, twin_ref, out_ref):
    half, units = keep_ref.shape
    rows = half // chips
    cases = 2 * half
    p1, p2 = stat_ref[0:1, :], swap_halves(twin_ref[0:1, :])
    t1, t2 = stat_ref[1:2, :], swap_halves(twin_ref[1:2, :])
    peak = jnp.maximum(p1, p2)
    env = peak + jnp.log(t1 * jnp.exp(p1 - peak) + t2 * jnp.exp(p2 - peak))
    lines = jnp.concatenate([env[:, at : at + 128] for at in range(0, cases, 128)], axis=0)
    high = lines.astype(jnp.bfloat16).astype(jnp.float32)
    middle = (lines - high).astype(jnp.bfloat16).astype(jnp.float32)
    low = lines - high - middle
    rest = jnp.zeros((16 - 3 * (cases // 128), 128), jnp.float32)
    tail = jnp.concatenate([high, middle, low, rest], axis=0).astype(jnp.bfloat16)
    g1, g2 = jnp.exp(p1 - env), jnp.exp(p2 - env)
    step = min(128, half)
    for at in range(0, half, step):
        up, down = to_rows(g1, at), to_rows(g2, at)
        for s in range(at // rows, (at + step) // rows):
            r = slice(s * rows, (s + 1) * rows)
            q = slice(s * rows - at, (s + 1) * rows - at)
            blocks = [
                keep_ref[r, c : c + 128] * up[q] + got_ref[r, c : c + 128].astype(jnp.float32) * down[q]
                for c in range(0, units, 128)
            ]
            value = jnp.concatenate(blocks, axis=0).astype(jnp.bfloat16)
            size = value.shape[0]
            out_ref[s, 0:size, :] = value
            out_ref[s, size : size + 16, :] = tail


def coef_kernel(me_ref, cot_ref, s_ref, w_ref, stat_ref, part_ref, coef_ref, gain_ref, turned):
    chips, size = part_ref.shape[0], part_ref.shape[1] - 16
    cases = cot_ref.shape[1]
    width = w_ref.shape[1]
    rows = cases // (2 * chips)
    groups = cases // 128
    envs = []
    for p in range(chips):
        lines = part_ref[p, size : size + 16, :].astype(jnp.float32)
        lines = lines[0:groups] + lines[groups : 2 * groups] + lines[2 * groups : 3 * groups]
        envs.append(jnp.concatenate([lines[g : g + 1] for g in range(groups)], axis=1))
    env_all = jnp.concatenate(envs, axis=0)
    top = jnp.max(env_all, axis=0, keepdims=True)
    env = top + jnp.log(jnp.sum(jnp.exp(env_all - top), axis=0, keepdims=True))
    cot = cot_ref[...]
    gain = cot * jnp.exp(env_all - env)
    pad = jnp.zeros((128 - chips, 128), jnp.float32)
    for at in range(0, cases // 2, 128):
        turned[at : at + 128, :] = jnp.transpose(jnp.concatenate([gain[:, at : at + 128], pad], axis=0))
    chip = me_ref[0] >> 1
    gain_ref[...] = turned[pl.ds(pl.multiple_of(chip * rows, rows), rows), :]
    mine = cot * jnp.exp(stat_ref[0:1, :] - env)
    scales = [to_rows(mine, at) for at in range(0, cases, 128)]
    for jb in range(width // JB):
        base = jb * 3 * JB
        for c in range(0, JB, 128):
            sums = [jnp.zeros((8, 128), jnp.float32) for _ in range(6)]
            for at in range(0, cases, 8):
                r = slice(at, at + 8)
                s1 = s_ref[r, base + c : base + c + 128]
                s2 = s_ref[r, base + JB + c : base + JB + c + 128]
                t = s_ref[r, base + 2 * JB + c : base + 2 * JB + c + 128]
                local = at % 128
                w = w_ref[r, jb * JB + c : jb * JB + c + 128] * scales[at // 128][local : local + 8]
                a, b = w * s1, w * s2
                for i, v in enumerate((a, b, a * s1, b * s2, w * t * t, a * s2)):
                    sums[i] = sums[i] + v
            for i in range(6):
                line = jnp.sum(sums[i], axis=0, keepdims=True)
                if i == 5:
                    line = 2.0 * line
                coef_ref[i : i + 1, jb * JB + c : jb * JB + c + 128] = line


def combine_kernel(gain_ref, part_ref, out_ref):
    rows, units = out_ref.shape
    chips = part_ref.shape[0]
    value = jnp.zeros((rows * units // 128, 128), jnp.float32)
    for p in range(chips):
        gain = jnp.broadcast_to(gain_ref[:, p : p + 1], (rows, 128))
        gain = jnp.concatenate([gain] * (units // 128), axis=0)
        value = value + part_ref[p, 0 : rows * units // 128, :].astype(jnp.float32) * gain
    for c in range(units // 128):
        out_ref[:, c * 128 : (c + 1) * 128] = value[c * rows : (c + 1) * rows]


def per_device(n, n_case, load_coef, mantissa, scale_exp, lin_coef, quad_coef, cross_coef, ply_count, cotangent):
    units, comps, width = mantissa.shape
    rows = load_coef.shape[0]
    cases = rows * n
    half, chips = cases // 2, n // 2
    f32, bf16 = jnp.float32, jnp.bfloat16
    shape = jax.ShapeDtypeStruct
    groups = [list(range(c, n, 2)) for c in range(2)]
    me = lax.axis_index("elem").astype(jnp.int32)

    def twin(x):
        return lax.ppermute(x, "elem", [(i, i ^ 1) for i in range(n)])

    copies = jnp.broadcast_to(load_coef[None], (chips, rows, units))
    mine = lax.all_to_all(copies, "elem", 0, 0, axis_index_groups=groups).reshape(half, units)
    other = twin(mine)
    cot = cotangent.reshape(chips, 2, rows)
    cot = jnp.concatenate(
        [lax.dynamic_index_in_dim(cot, (me & 1) ^ c, 1, keepdims=False).reshape(1, half) for c in range(2)], axis=1
    )

    fields, cot = vmem_call(
        prep_kernel,
        [shape((units, comps * width), bf16), shape((1, cases), f32)],
        flops=units * comps * width,
        nbytes=4 * units * comps * width,
        n_in=3,
    )(jnp.transpose(mantissa, (1, 0, 2)), jnp.transpose(scale_exp, (1, 2, 0)), cot)

    keep, send, stat, stress, weight = vmem_call(
        main_kernel,
        [
            shape((half, units), f32),
            shape((half, units), bf16),
            shape((2, cases), f32),
            shape((cases, comps * width), f32),
            shape((cases, width), f32),
        ],
        scratch_shapes=[
            VMEM((cases, width), f32),
            VMEM((cases, comps * width), bf16),
            VMEM((cases, units), f32),
        ],
        flops=4 * cases * units * comps * width,
        nbytes=2 * units * comps * width + 4 * cases * 4 * width,
        exps=cases * width,
        n_in=7,
        limit=24,
    )(mine, other, fields, lin_coef, quad_coef, cross_coef.reshape(1, width), ply_count.reshape(1, width))

    chunks = vmem_call(
        functools.partial(merge_kernel, chips),
        shape((chips, rows * units // 128 + 16, 128), bf16),
        flops=4 * half * units,
        nbytes=8 * half * units,
        n_in=4,
    )(keep, twin(send), stat, twin(stat))
    parts = lax.all_to_all(chunks, "elem", 0, 0, axis_index_groups=groups)

    coef, gain = vmem_call(
        coef_kernel,
        [shape((6, width), f32), shape((rows, 128), f32)],
        scratch_shapes=[VMEM((half, 128), f32)],
        flops=14 * cases * width,
        nbytes=16 * cases * width,
        n_in=6,
        smem=(0,),
    )(me.reshape(1), cot, stress, weight, stat, parts)
    bit = 1
    while bit < n_case:
        coef = coef + lax.ppermute(coef, "case", [(i, i ^ bit) for i in range(n_case)])
        bit *= 2

    load_grad = vmem_call(
        combine_kernel,
        shape((rows, units), f32),
        flops=2 * n * rows * units,
        nbytes=2 * n * rows * units,
        n_in=2,
    )(gain, parts)
    return (load_grad, coef)


def solution(mesh):
    n, n_case = mesh.shape["elem"], mesh.shape["case"]
    return jax.shard_map(
        functools.partial(per_device, n, n_case),
        mesh=mesh,
        in_specs=(
            P(("case", "elem"), None),
            P(None, None, "elem"),
            P(None, None, "elem"),
            P(None, "elem"),
            P(None, "elem"),
            P("elem"),
            P("elem"),
            P("case"),
        ),
        out_specs=(P(("case", "elem"), None), P(None, "elem")),
        check_vma=False,
    )
```

```python
import functools

import jax
import jax.numpy as jnp
from jax import lax
from jax.experimental import pallas as pl
from jax.experimental.pallas import tpu as pltpu
from jax.sharding import PartitionSpec as P

JB = 256
VMEM = pltpu.VMEM


def vmem_call(kernel, out_shape, scratch_shapes=(), flops=0, nbytes=0, exps=0, n_in=0, smem=(), hbm=(), limit=16):
    def place(i):
        return pltpu.SMEM if i in smem else pltpu.HBM if i in hbm else VMEM

    return pl.pallas_call(
        kernel,
        out_shape=out_shape,
        in_specs=[pl.BlockSpec(memory_space=place(i)) for i in range(n_in)],
        out_specs=jax.tree.map(lambda _: pl.BlockSpec(memory_space=VMEM), out_shape),
        scratch_shapes=list(scratch_shapes),
        cost_estimate=pl.CostEstimate(flops=flops, bytes_accessed=nbytes, transcendentals=exps),
        compiler_params=pltpu.CompilerParams(vmem_limit_bytes=limit << 20),
    )


def to_lanes(column, rows):
    step = min(rows, 128)
    parts = []
    for at in range(0, rows, step):
        square = jnp.broadcast_to(column[at : at + step], (step, 128))
        parts.append(jnp.transpose(square)[0:1, :])
    return jnp.concatenate(parts, axis=1)


def to_rows(row, at):
    return jnp.transpose(jnp.broadcast_to(row[:, at : at + 128], (128, 128)))


def swap_lanes(x, which, width, n):
    lane = lax.broadcasted_iota(jnp.int32, x.shape, 1)
    bit = 1
    while bit < n:
        step = bit * width
        ahead = jnp.concatenate([x[:, step:], x[:, :step]], axis=1)
        behind = jnp.concatenate([x[:, -step:], x[:, :-step]], axis=1)
        other = jnp.where((lane & step) != 0, behind, ahead)
        x = jnp.where((which & bit) != 0, other, x)
        bit *= 2
    return x


def swap_halves(x):
    half = x.shape[1] // 2
    return jnp.concatenate([x[:, half:], x[:, :half]], axis=1)


def pair_kernel(core_ref, own_ref, twin_ref, out_ref):
    own, twin = own_ref[...].astype(jnp.float32), twin_ref[...].astype(jnp.float32)

    @pl.when(core_ref[0] == 0)
    def _():
        out_ref[...] = jnp.concatenate([own, twin], axis=0).astype(jnp.bfloat16)

    @pl.when(core_ref[0] != 0)
    def _():
        out_ref[...] = jnp.concatenate([twin, own], axis=0).astype(jnp.bfloat16)


def prep_kernel(chip_ref, mant_hbm, exp_ref, cot_ref, out_ref, cot_out_ref, mant, sems):
    comps, units, width = mant.shape
    blocks = exp_ref.shape[1]
    span = width // blocks
    copies = [pltpu.make_async_copy(mant_hbm.at[k], mant.at[k], sems.at[k]) for k in range(comps)]
    for copy in copies:
        copy.start()
    chips = cot_ref.shape[0]
    order = list(range(0, chips, 2)) + list(range(1, chips, 2))
    cot_out_ref[...] = jnp.concatenate([cot_ref[pl.ds(chip_ref[0] ^ p, 1), :] for p in order], axis=1)
    factor = jnp.exp2(exp_ref[...].astype(jnp.float32)).reshape(comps * blocks, units)
    pad = jnp.zeros((128 - comps * blocks, units), jnp.float32)
    columns = jnp.transpose(jnp.concatenate([factor, pad], axis=0))
    for k in range(comps):
        copies[k].wait()
        for b in range(blocks):
            gain = jnp.broadcast_to(columns[:, k * blocks + b : k * blocks + b + 1], (units, span))
            value = mant[k, :, b * span : (b + 1) * span] * gain.astype(jnp.bfloat16)
            first = b * span
            at = (first // JB) * (comps * JB) + k * JB + first % JB
            out_ref[:, at : at + span] = value


def main_kernel(f_ref, lin_ref, quad_ref, cross_ref, ply_ref, *refs):
    keep_ref, send_ref, stat_ref, s_ref, w_ref, a_ref, idx, d, acc = refs[-9:]
    half = keep_ref.shape[0]
    cases = 2 * half
    at = 0
    for ref in refs[:-9]:
        a_ref[at : at + ref.shape[0], :] = ref[...]
        at += ref.shape[0]
    width = lin_ref.shape[1]
    tile = 32
    peak = jnp.full((cases, 128), -jnp.inf, jnp.float32)
    for jb in range(width // JB):
        cols = slice(jb * JB, (jb + 1) * JB)
        base = jb * 3 * JB
        s_ref[:, base : base + 3 * JB] = jnp.dot(
            a_ref[...], f_ref[:, base : base + 3 * JB], preferred_element_type=jnp.float32
        )
        f1, f2 = lin_ref[0:1, cols], lin_ref[1:2, cols]
        f11, f22, f66 = quad_ref[0:1, cols], quad_ref[1:2, cols], quad_ref[2:3, cols]
        f12 = 2.0 * cross_ref[0:1, cols]
        tops = []
        for at in range(0, cases, tile):
            r = slice(at, at + tile)
            s1 = s_ref[r, base : base + JB]
            s2 = s_ref[r, base + JB : base + 2 * JB]
            t = s_ref[r, base + 2 * JB : base + 3 * JB]
            index = s1 * (f1 + f11 * s1 + f12 * s2) + s2 * (f2 + f22 * s2) + f66 * (t * t)
            idx[r, cols] = index
            top = index[:, 0:128]
            for c in range(128, JB, 128):
                top = jnp.maximum(top, index[:, c : c + 128])
            tops.append(top)
        peak = jnp.maximum(peak, jnp.concatenate(tops, axis=0))
    peak = jnp.max(peak, axis=1, keepdims=True)

    total = jnp.zeros((cases, 128), jnp.float32)
    for jb in range(width // JB):
        cols = slice(jb * JB, (jb + 1) * JB)
        base = jb * 3 * JB
        f1, f2 = lin_ref[0:1, cols], lin_ref[1:2, cols]
        q11, q22, q66 = 2.0 * quad_ref[0:1, cols], 2.0 * quad_ref[1:2, cols], 2.0 * quad_ref[2:3, cols]
        f12 = 2.0 * cross_ref[0:1, cols]
        plies = (ply_ref[0:1, cols] + 1).astype(jnp.float32)
        sums = []
        for at in range(0, cases, tile):
            r = slice(at, at + tile)
            s1 = s_ref[r, base : base + JB]
            s2 = s_ref[r, base + JB : base + 2 * JB]
            t = s_ref[r, base + 2 * JB : base + 3 * JB]
            w = plies * jnp.exp(idx[r, cols] - peak[r])
            w_ref[r, cols] = w
            part = w[:, 0:128]
            for c in range(128, JB, 128):
                part = part + w[:, c : c + 128]
            sums.append(part)
            d[r, base : base + JB] = (w * (f1 + q11 * s1 + f12 * s2)).astype(jnp.bfloat16)
            d[r, base + JB : base + 2 * JB] = (w * (f2 + q22 * s2 + f12 * s1)).astype(jnp.bfloat16)
            d[r, base + 2 * JB : base + 3 * JB] = (w * (q66 * t)).astype(jnp.bfloat16)
        total = total + jnp.concatenate(sums, axis=0)
        part = lax.dot_general(
            d[:, base : base + 3 * JB],
            f_ref[:, base : base + 3 * JB],
            (((1,), (1,)), ((), ())),
            preferred_element_type=jnp.float32,
        )
        if jb == 0:
            acc[...] = part
        elif jb < width // JB - 1:
            acc[...] += part
        else:
            keep_ref[...] = acc[0:half] + part[0:half]
            send_ref[...] = (acc[half:] + part[half:]).astype(jnp.bfloat16)
    total = jnp.sum(total, axis=1, keepdims=True)
    stat_ref[0:1, :] = to_lanes(peak, cases)
    stat_ref[1:2, :] = to_lanes(total, cases)


def merge_kernel(keep_ref, got_ref, stat_ref, twin_ref, *out_refs):
    half, units = keep_ref.shape
    rows = half // len(out_refs)
    cases = 2 * half
    p1, p2 = stat_ref[0:1, :], swap_halves(twin_ref[0:1, :])
    t1, t2 = stat_ref[1:2, :], swap_halves(twin_ref[1:2, :])
    peak = jnp.maximum(p1, p2)
    env = peak + jnp.log(t1 * jnp.exp(p1 - peak) + t2 * jnp.exp(p2 - peak))
    lines = jnp.concatenate([env[:, at : at + 128] for at in range(0, cases, 128)], axis=0)
    high = lines.astype(jnp.bfloat16).astype(jnp.float32)
    middle = (lines - high).astype(jnp.bfloat16).astype(jnp.float32)
    low = lines - high - middle
    rest = jnp.zeros((16 - 3 * (cases // 128), 128), jnp.float32)
    tail = jnp.concatenate([high, middle, low, rest], axis=0).astype(jnp.bfloat16)
    g1, g2 = jnp.exp(p1 - env), jnp.exp(p2 - env)
    step = min(128, half)
    for at in range(0, half, step):
        up, down = to_rows(g1, at), to_rows(g2, at)
        for j in range(at // rows, (at + step) // rows):
            r = slice(j * rows, (j + 1) * rows)
            q = slice(j * rows - at, (j + 1) * rows - at)
            blocks = [
                keep_ref[r, c : c + 128] * up[q] + got_ref[r, c : c + 128].astype(jnp.float32) * down[q]
                for c in range(0, units, 128)
            ]
            value = jnp.concatenate(blocks, axis=0).astype(jnp.bfloat16)
            size = value.shape[0]
            out_refs[j][0:size, :] = value
            out_refs[j][size : size + 16, :] = tail


def coef_kernel(core_ref, cot_ref, s_ref, w_ref, stat_ref, *refs):
    coef_ref, gain_ref = refs[-2:]
    part_refs = refs[:-2]
    count = len(part_refs) // 2
    size = part_refs[0].shape[0] - 16
    cases = cot_ref.shape[1]
    width = w_ref.shape[1]
    groups = cases // 128
    rows = cases // (2 * count)
    envs = []
    for ref in part_refs:
        lines = ref[size : size + 16, :].astype(jnp.float32)
        lines = lines[0:groups] + lines[groups : 2 * groups] + lines[2 * groups : 3 * groups]
        envs.append(jnp.concatenate([lines[g : g + 1] for g in range(groups)], axis=1))
    env_all = jnp.concatenate(envs, axis=0)
    which = lax.broadcasted_iota(jnp.int32, env_all.shape, 0) & (count - 1)
    env_all = swap_lanes(env_all, which, rows, count)
    top = jnp.max(env_all, axis=0, keepdims=True)
    env = top + jnp.log(jnp.sum(jnp.exp(env_all - top), axis=0, keepdims=True))
    cot = cot_ref[...]
    gain = cot[:, 0:128] * jnp.exp(env_all[:, 0:128] - env[:, 0:128])
    pad = jnp.zeros((128 - 2 * count, 128), jnp.float32)
    gain_ref[...] = jnp.transpose(jnp.concatenate([gain, pad], axis=0))[0:rows]
    both = jnp.concatenate([cot, env], axis=0)
    both = jnp.where(core_ref[0] == 0, both, swap_halves(both))
    mine = both[0:1] * jnp.exp(stat_ref[0:1, :] - both[1:2])
    scales = [to_rows(mine, at) for at in range(0, cases, 128)]
    for jb in range(width // JB):
        base = jb * 3 * JB
        for c in range(0, JB, 128):
            sums = [jnp.zeros((8, 128), jnp.float32) for _ in range(6)]
            for at in range(0, cases, 8):
                r = slice(at, at + 8)
                s1 = s_ref[r, base + c : base + c + 128]
                s2 = s_ref[r, base + JB + c : base + JB + c + 128]
                t = s_ref[r, base + 2 * JB + c : base + 2 * JB + c + 128]
                local = at % 128
                w = w_ref[r, jb * JB + c : jb * JB + c + 128] * scales[at // 128][local : local + 8]
                a, b = w * s1, w * s2
                for i, v in enumerate((a, b, a * s1, b * s2, w * t * t, a * s2)):
                    sums[i] = sums[i] + v
            for i in range(6):
                line = jnp.sum(sums[i], axis=0, keepdims=True)
                if i == 5:
                    line = 2.0 * line
                coef_ref[i : i + 1, jb * JB + c : jb * JB + c + 128] = line


def combine_kernel(core_ref, gain_ref, *refs):
    part_refs, out_ref, total = refs[:-2], refs[-2], refs[-1]
    rows, units = out_ref.shape
    value = jnp.zeros(total.shape, jnp.float32)
    for p, ref in enumerate(part_refs):
        gain = jnp.broadcast_to(gain_ref[:, p : p + 1], (2 * rows, 128))
        gain = jnp.concatenate([gain] * (units // 128), axis=0)
        value = value + ref[0 : total.shape[0], :].astype(jnp.float32) * gain
    total[...] = value
    for c in range(units // 128):
        at = pl.multiple_of((2 * c + core_ref[0]) * rows, rows)
        out_ref[:, c * 128 : (c + 1) * 128] = total[pl.ds(at, rows), :]


def per_device(n, n_case, load_coef, mantissa, scale_exp, lin_coef, quad_coef, cross_coef, ply_count, cotangent):
    units, comps, width = mantissa.shape
    rows = load_coef.shape[0]
    cases = rows * n
    half, chips = cases // 2, n // 2
    count = chips // 2
    f32, bf16 = jnp.float32, jnp.bfloat16
    shape = jax.ShapeDtypeStruct
    me = lax.axis_index("elem").astype(jnp.int32)
    core, chip = (me & 1).reshape(1), (me >> 1).reshape(1)

    def twin(x):
        return lax.ppermute(x, "elem", [(i, i ^ 1) for i in range(n)])

    def reach(x, j):
        return lax.ppermute(x, "elem", [(i, ((i >> 1) ^ (2 * j + (i & 1))) * 2 + (i & 1)) for i in range(n)])

    block = vmem_call(
        pair_kernel, shape((2 * rows, units), bf16), nbytes=8 * rows * units, n_in=3, smem=(0,)
    )(core, load_coef, twin(load_coef))
    mine = [reach(block, j) for j in range(count)]
    fields, cot = vmem_call(
        prep_kernel,
        [shape((units, comps * width), bf16), shape((1, cases), f32)],
        scratch_shapes=[VMEM((comps, units, width), bf16), pltpu.SemaphoreType.DMA((comps,))],
        flops=units * comps * width,
        nbytes=4 * units * comps * width,
        n_in=4,
        smem=(0,),
        hbm=(1,),
    )(
        chip,
        pltpu.with_memory_space_constraint(jnp.transpose(mantissa, (1, 0, 2)), pltpu.HBM),
        jnp.transpose(scale_exp, (1, 2, 0)),
        cotangent.reshape(chips, 2 * rows),
    )

    mine[0], fields = lax.optimization_barrier((mine[0], fields))
    other = [twin(x) for x in mine]

    keep, send, stat, stress, weight = vmem_call(
        main_kernel,
        [
            shape((half, units), f32),
            shape((half, units), bf16),
            shape((2, cases), f32),
            shape((cases, comps * width), f32),
            shape((cases, width), f32),
        ],
        scratch_shapes=[
            VMEM((cases, units), bf16),
            VMEM((cases, width), f32),
            VMEM((cases, comps * width), bf16),
            VMEM((cases, units), f32),
        ],
        flops=4 * cases * units * comps * width,
        nbytes=2 * units * comps * width + 4 * cases * 4 * width,
        exps=cases * width,
        n_in=5 + 2 * count,
        limit=24,
    )(fields, lin_coef, quad_coef, cross_coef.reshape(1, width), ply_count.reshape(1, width), *mine, *other)

    chunks = vmem_call(
        merge_kernel,
        [shape((2 * rows * units // 128 + 16, 128), bf16)] * count,
        flops=4 * half * units,
        nbytes=8 * half * units,
        n_in=4,
    )(keep, twin(send), stat, twin(stat))
    parts = [reach(x, j) for j, x in enumerate(chunks)]
    parts = parts + [twin(x) for x in parts]

    coef, gain = vmem_call(
        coef_kernel,
        [shape((6, width), f32), shape((2 * rows, 128), f32)],
        flops=14 * cases * width,
        nbytes=16 * cases * width,
        n_in=5 + chips,
        smem=(0,),
    )(core, cot, stress, weight, stat, *parts)
    bit = 1
    while bit < n_case:
        coef = coef + lax.ppermute(coef, "case", [(i, i ^ bit) for i in range(n_case)])
        bit *= 2

    load_grad = vmem_call(
        combine_kernel,
        shape((rows, units), f32),
        scratch_shapes=[VMEM((2 * rows * units // 128, 128), f32)],
        flops=2 * n * rows * units,
        nbytes=2 * n * rows * units,
        n_in=2 + chips,
        smem=(0,),
    )(core, gain, *parts)
    return (load_grad, coef)


def solution(mesh):
    n, n_case = mesh.shape["elem"], mesh.shape["case"]
    return jax.shard_map(
        functools.partial(per_device, n, n_case),
        mesh=mesh,
        in_specs=(
            P(("case", "elem"), None),
            P(None, None, "elem"),
            P(None, None, "elem"),
            P(None, "elem"),
            P(None, "elem"),
            P("elem"),
            P("elem"),
            P("case"),
        ),
        out_specs=(P(("case", "elem"), None), P(None, "elem")),
        check_vma=False,
    )
```

```python
import functools

import jax
import jax.numpy as jnp
from jax import lax
from jax.experimental import pallas as pl
from jax.experimental.pallas import tpu as pltpu
from jax.sharding import PartitionSpec as P

JB = 256
VMEM = pltpu.VMEM


def vmem_call(kernel, out_shape, scratch_shapes=(), flops=0, nbytes=0, exps=0, n_in=0, smem=(), hbm=(), limit=16):
    def place(i):
        return pltpu.SMEM if i in smem else pltpu.HBM if i in hbm else VMEM

    return pl.pallas_call(
        kernel,
        out_shape=out_shape,
        in_specs=[pl.BlockSpec(memory_space=place(i)) for i in range(n_in)],
        out_specs=jax.tree.map(lambda _: pl.BlockSpec(memory_space=VMEM), out_shape),
        scratch_shapes=list(scratch_shapes),
        cost_estimate=pl.CostEstimate(flops=flops, bytes_accessed=nbytes, transcendentals=exps),
        compiler_params=pltpu.CompilerParams(vmem_limit_bytes=limit << 20),
    )


def to_lanes(column, rows):
    step = min(rows, 128)
    parts = []
    for at in range(0, rows, step):
        square = jnp.broadcast_to(column[at : at + step], (step, 128))
        parts.append(jnp.transpose(square)[0:1, :])
    return jnp.concatenate(parts, axis=1)


def to_rows(row, at):
    return jnp.transpose(jnp.broadcast_to(row[:, at : at + 128], (128, 128)))


def swap_lanes(x, which, width, n):
    lane = lax.broadcasted_iota(jnp.int32, x.shape, 1)
    bit = 1
    while bit < n:
        step = bit * width
        ahead = jnp.concatenate([x[:, step:], x[:, :step]], axis=1)
        behind = jnp.concatenate([x[:, -step:], x[:, :-step]], axis=1)
        other = jnp.where((lane & step) != 0, behind, ahead)
        x = jnp.where((which & bit) != 0, other, x)
        bit *= 2
    return x


def swap_halves(x):
    half = x.shape[1] // 2
    return jnp.concatenate([x[:, half:], x[:, :half]], axis=1)


def block_kernel(*refs):
    out_ref = refs[-1]
    values = [ref[...].astype(jnp.float32) for ref in refs[:-1]]
    out_ref[...] = jnp.concatenate(values, axis=0).astype(jnp.bfloat16)


def prep_kernel(n, me_ref, mant_hbm, exp_hbm, cot_ref, out_ref, cot_out_ref, mant, expo, sems):
    comps, units, width = mant.shape
    blocks = expo.shape[1]
    span = width // blocks
    copies = [pltpu.make_async_copy(exp_hbm, expo, sems.at[comps])]
    copies += [pltpu.make_async_copy(mant_hbm.at[k], mant.at[k], sems.at[k]) for k in range(comps)]
    for copy in copies:
        copy.start()
    cases = cot_ref.shape[1]
    rows = cases // n
    nz = n // 4
    order = [z * 4 + y * 2 + c for c in range(2) for y in range(2) for z in range(nz)]
    cot = jnp.concatenate([cot_ref[:, e * rows : (e + 1) * rows] for e in order], axis=1)
    code = (me_ref[0] & 1) * (2 * nz) + ((me_ref[0] >> 1) & 1) * nz + (me_ref[0] >> 2)
    cot = jnp.broadcast_to(cot, (8, cases))
    cot_out_ref[...] = swap_lanes(cot, jnp.full((8, cases), code, jnp.int32), rows, n)[0:1]
    copies[0].wait()
    factor = jnp.exp2(expo[...].astype(jnp.float32)).reshape(comps * blocks, units)
    pad = jnp.zeros((128 - comps * blocks, units), jnp.float32)
    columns = jnp.transpose(jnp.concatenate([factor, pad], axis=0))
    for k in range(comps):
        copies[1 + k].wait()
        for b in range(blocks):
            gain = jnp.broadcast_to(columns[:, k * blocks + b : k * blocks + b + 1], (units, span))
            value = mant[k, :, b * span : (b + 1) * span] * gain.astype(jnp.bfloat16)
            first = b * span
            at = (first // JB) * (comps * JB) + k * JB + first % JB
            out_ref[:, at : at + span] = value


def main_kernel(n_rows, n_stat, f_ref, lin_ref, quad_ref, cross_ref, ply_ref, *refs):
    row_refs, stat_refs = refs[:n_rows], refs[n_rows : n_rows + n_stat]
    term_refs = refs[n_rows + n_stat : 2 * n_rows + n_stat]
    stat_ref, s_ref, w_ref, a_ref, idx, d, acc = refs[2 * n_rows + n_stat :]
    cases = a_ref.shape[0]
    width = w_ref.shape[1]
    at = 0
    for ref in row_refs:
        a_ref[at : at + ref.shape[0], :] = ref[...]
        at += ref.shape[0]
    tile = 32
    peak = jnp.full((cases, 128), -jnp.inf, jnp.float32)
    for jb in range(width // JB):
        cols = slice(jb * JB, (jb + 1) * JB)
        base = jb * 3 * JB
        s_ref[:, base : base + 3 * JB] = jnp.dot(
            a_ref[...], f_ref[:, base : base + 3 * JB], preferred_element_type=jnp.float32
        )
        f1, f2 = lin_ref[0:1, cols], lin_ref[1:2, cols]
        f11, f22, f66 = quad_ref[0:1, cols], quad_ref[1:2, cols], quad_ref[2:3, cols]
        f12 = 2.0 * cross_ref[0:1, cols]
        tops = []
        for at in range(0, cases, tile):
            r = slice(at, at + tile)
            s1 = s_ref[r, base : base + JB]
            s2 = s_ref[r, base + JB : base + 2 * JB]
            t = s_ref[r, base + 2 * JB : base + 3 * JB]
            index = s1 * (f1 + f11 * s1 + f12 * s2) + s2 * (f2 + f22 * s2) + f66 * (t * t)
            idx[r, cols] = index
            top = index[:, 0:128]
            for c in range(128, JB, 128):
                top = jnp.maximum(top, index[:, c : c + 128])
            tops.append(top)
        peak = jnp.maximum(peak, jnp.concatenate(tops, axis=0))
    peak = jnp.max(peak, axis=1, keepdims=True)

    total = jnp.zeros((cases, 128), jnp.float32)
    for jb in range(width // JB):
        cols = slice(jb * JB, (jb + 1) * JB)
        base = jb * 3 * JB
        f1, f2 = lin_ref[0:1, cols], lin_ref[1:2, cols]
        q11, q22, q66 = 2.0 * quad_ref[0:1, cols], 2.0 * quad_ref[1:2, cols], 2.0 * quad_ref[2:3, cols]
        f12 = 2.0 * cross_ref[0:1, cols]
        plies = (ply_ref[0:1, cols] + 1).astype(jnp.float32)
        sums = []
        for at in range(0, cases, tile):
            r = slice(at, at + tile)
            s1 = s_ref[r, base : base + JB]
            s2 = s_ref[r, base + JB : base + 2 * JB]
            t = s_ref[r, base + 2 * JB : base + 3 * JB]
            w = plies * jnp.exp(idx[r, cols] - peak[r])
            w_ref[r, cols] = w
            part = w[:, 0:128]
            for c in range(128, JB, 128):
                part = part + w[:, c : c + 128]
            sums.append(part)
            d[r, base : base + JB] = (w * (f1 + q11 * s1 + f12 * s2)).astype(jnp.bfloat16)
            d[r, base + JB : base + 2 * JB] = (w * (f2 + q22 * s2 + f12 * s1)).astype(jnp.bfloat16)
            d[r, base + 2 * JB : base + 3 * JB] = (w * (q66 * t)).astype(jnp.bfloat16)
        total = total + jnp.concatenate(sums, axis=0)
        part = lax.dot_general(
            d[:, base : base + 3 * JB],
            f_ref[:, base : base + 3 * JB],
            (((1,), (1,)), ((), ())),
            preferred_element_type=jnp.float32,
        )
        if jb == 0:
            acc[...] = part
        elif jb < width // JB - 1:
            acc[...] += part
        else:
            total = jnp.sum(total, axis=1, keepdims=True)
            part = (acc[...] + part) * (1.0 / total)
            at = 0
            for ref in term_refs:
                ref[...] = part[at : at + ref.shape[0]].astype(ref.dtype)
                at += ref.shape[0]
    lines = [to_lanes(peak, cases), to_lanes(peak + jnp.log(total), cases)]
    at = 0
    for ref in stat_refs:
        at += ref.shape[1]
    if stat_refs:
        quarter = cases
        first, second = stat_refs
        stat_ref[:, 0:quarter] = first[:, 0:quarter]
        stat_ref[:, quarter : 2 * quarter] = second[...]
        stat_ref[:, 2 * quarter : 3 * quarter] = first[:, quarter : 2 * quarter]
        at = 3 * quarter
    stat_ref[0:1, at : at + cases] = lines[0]
    stat_ref[1:2, at : at + cases] = lines[1]


def join(a, b):
    top = jnp.maximum(a, b)
    return top + jnp.log(jnp.exp(a - top) + jnp.exp(b - top))


def encode(env):
    groups = env.shape[1] // 128
    lines = jnp.concatenate([env[:, g * 128 : (g + 1) * 128] for g in range(groups)], axis=0)
    high = lines.astype(jnp.bfloat16).astype(jnp.float32)
    middle = (lines - high).astype(jnp.bfloat16).astype(jnp.float32)
    rest = jnp.zeros((16 - 3 * groups, 128), jnp.float32)
    return jnp.concatenate([high, middle, lines - high - middle, rest], axis=0).astype(jnp.bfloat16)


def decode(ref, cases):
    size, groups = ref.shape[0] - 16, cases // 128
    lines = ref[size : size + 16, :].astype(jnp.float32)
    lines = lines[0:groups] + lines[groups : 2 * groups] + lines[2 * groups : 3 * groups]
    return jnp.concatenate([lines[g : g + 1] for g in range(groups)], axis=1)


def fold(x):
    return jnp.concatenate([x[:, c : c + 128] for c in range(0, x.shape[1], 128)], axis=0)


def cores_kernel(own_ref, got_ref, stat_ref, twin_ref, out_ref):
    quarter = own_ref.shape[0]
    cases = 4 * quarter
    mine, theirs = stat_ref[1:2, :], swap_halves(twin_ref[1:2, :])
    env = join(mine, theirs)
    r = slice(quarter, 2 * quarter)
    up = column(jnp.exp(mine - env)[:, r], quarter)
    down = column(jnp.exp(theirs - env)[:, r], quarter)
    value = own_ref[...] * up + got_ref[...].astype(jnp.float32) * down
    size = out_ref.shape[0] - 16
    out_ref[0:size, :] = fold(value).astype(jnp.bfloat16)
    out_ref[size : size + 16, :] = encode(env)


def column(row, rows):
    return jnp.concatenate([to_rows(row, at)[:, 0:1] for at in range(0, rows, 128)], axis=0)


def chips_kernel(own_ref, got_ref, stat_ref, twin_ref, part_ref, own_out_ref, env_ref, *out_refs):
    quarter, units = own_ref.shape
    cases = 4 * quarter
    rows = quarter // (1 + len(out_refs))
    mine, theirs = stat_ref[1:2, :], swap_halves(twin_ref[1:2, :])
    far = decode(part_ref, cases)
    far = jnp.concatenate([far[:, g * quarter : (g + 1) * quarter] for g in (1, 0, 3, 2)], axis=1)
    env = join(join(mine, theirs), far)
    env_ref[...] = env
    scale = [column(jnp.exp(x - env)[:, 0:quarter], quarter) for x in (mine, theirs, far)]
    total = own_ref[...] * scale[0] + got_ref[...].astype(jnp.float32) * scale[1]
    parts = []
    for c in range(units // 128):
        part = part_ref[c * quarter : (c + 1) * quarter, :].astype(jnp.float32)
        parts.append(total[:, c * 128 : (c + 1) * 128] + part * scale[2])
    own_out_ref[...] = jnp.concatenate([p[0:rows] for p in parts], axis=0)
    tail = encode(env)
    for m, ref in enumerate(out_refs):
        r = slice((m + 1) * rows, (m + 2) * rows)
        size = ref.shape[0] - 16
        ref[0:size, :] = jnp.concatenate([p[r] for p in parts], axis=0).astype(jnp.bfloat16)
        ref[size : size + 16, :] = tail


def coef_kernel(cot_ref, stat_ref, env_ref, s0_ref, s1_ref, s2_ref, w0_ref, w1_ref, w2_ref, *refs):
    coef_ref, gain_ref = refs[-2:]
    part_refs = refs[:-2]
    nz = 1 + len(part_refs)
    cases = cot_ref.shape[1]
    quarter = cases // 4
    rows = quarter // nz
    width = w0_ref.shape[1]
    envs = [env_ref[...]] + [decode(ref, cases) for ref in part_refs]
    pad = -nz % 8
    env_all = jnp.concatenate(envs + [envs[0]] * pad, axis=0)
    which = lax.broadcasted_iota(jnp.int32, env_all.shape, 0)
    env_all = swap_lanes(env_all, jnp.where(which < nz, which, 0), rows, nz)[0:nz]
    top = jnp.max(env_all, axis=0, keepdims=True)
    env = top + jnp.log(jnp.sum(jnp.exp(env_all - top), axis=0, keepdims=True))
    cot = cot_ref[...]
    gain = cot[:, 0:128] * jnp.exp(env_all[:, 0:128] - env[:, 0:128])
    fill = jnp.zeros((128 - nz, 128), jnp.float32)
    gain_ref[...] = jnp.transpose(jnp.concatenate([gain, fill], axis=0))[0:rows]
    scale = cot * jnp.exp(stat_ref[0:1, :] - env)
    scales = [to_rows(scale, at) for at in range(0, cases, 128)]
    sets = [
        (0, s0_ref, w0_ref, 0),
        (quarter, s1_ref, w1_ref, 0),
        (2 * quarter, s0_ref, w0_ref, quarter),
        (3 * quarter, s2_ref, w2_ref, 0),
    ]
    for jb in range(width // JB):
        base = jb * 3 * JB
        for c in range(0, JB, 128):
            sums = [jnp.zeros((8, 128), jnp.float32) for _ in range(6)]
            for here, s_ref, w_ref, there in sets:
                for at in range(0, quarter, 8):
                    r = slice(there + at, there + at + 8)
                    s1 = s_ref[r, base + c : base + c + 128]
                    s2 = s_ref[r, base + JB + c : base + JB + c + 128]
                    t = s_ref[r, base + 2 * JB + c : base + 2 * JB + c + 128]
                    place = here + at
                    gain = scales[place // 128][place % 128 : place % 128 + 8]
                    w = w_ref[r, jb * JB + c : jb * JB + c + 128] * gain
                    a, b = w * s1, w * s2
                    for i, v in enumerate((a, b, a * s1, b * s2, w * t * t, a * s2)):
                        sums[i] = sums[i] + v
            for i in range(6):
                line = jnp.sum(sums[i], axis=0, keepdims=True)
                if i == 5:
                    line = 2.0 * line
                coef_ref[i : i + 1, jb * JB + c : jb * JB + c + 128] = line


def combine_kernel(gain_ref, own_ref, *refs):
    part_refs, out_ref = refs[:-1], refs[-1]
    rows, units = out_ref.shape
    size = rows * units // 128
    for c in range(units // 128):
        r = slice(c * rows, (c + 1) * rows)
        value = own_ref[r, :] * gain_ref[:, 0:1]
        for m, ref in enumerate(part_refs):
            part = ref[0:size, :].astype(jnp.float32)[r]
            value = value + part * gain_ref[:, m + 1 : m + 2]
        out_ref[:, c * 128 : (c + 1) * 128] = value


def per_device(n, n_case, load_coef, mantissa, scale_exp, lin_coef, quad_coef, cross_coef, ply_count, cotangent):
    units, comps, width = mantissa.shape
    rows = load_coef.shape[0]
    cases = rows * n
    nz = n // 4
    quarter = rows * nz
    f32, bf16 = jnp.float32, jnp.bfloat16
    shape = jax.ShapeDtypeStruct
    me = lax.axis_index("elem").astype(jnp.int32).reshape(1)

    def along(bits, x):
        return lax.ppermute(x, "elem", [(i, i ^ bits) for i in range(n)])

    along_z = [along(4 * m, load_coef) for m in range(1, nz)]
    fields, cot = vmem_call(
        functools.partial(prep_kernel, n),
        [shape((units, comps * width), bf16), shape((1, cases), f32)],
        scratch_shapes=[
            VMEM((comps, units, width), bf16),
            VMEM((comps, scale_exp.shape[2], units), jnp.int32),
            pltpu.SemaphoreType.DMA((comps + 1,)),
        ],
        flops=units * comps * width,
        nbytes=4 * units * comps * width,
        n_in=4,
        smem=(0,),
        hbm=(1, 2),
    )(
        me,
        pltpu.with_memory_space_constraint(jnp.transpose(mantissa, (1, 0, 2)), pltpu.HBM),
        pltpu.with_memory_space_constraint(jnp.transpose(scale_exp, (1, 2, 0)), pltpu.HBM),
        cotangent.reshape(1, cases),
    )
    along_z[0], fields = lax.optimization_barrier((along_z[0], fields))
    near = vmem_call(block_kernel, shape((quarter, units), bf16), nbytes=4 * quarter * units, n_in=nz)(
        load_coef, *along_z
    )
    far = along(2, near)
    near_twin, far_twin = along(1, near), along(1, far)

    def main(blocks, dtypes, stats=()):
        count = len(blocks) * quarter
        outs = vmem_call(
            functools.partial(main_kernel, len(blocks), len(stats)),
            [shape((quarter, units), dtype) for dtype in dtypes]
            + [
                shape((2, cases if stats else count), f32),
                shape((count, comps * width), f32),
                shape((count, width), f32),
            ],
            scratch_shapes=[
                VMEM((count, units), bf16),
                VMEM((count, width), f32),
                VMEM((count, comps * width), bf16),
                VMEM((count, units), f32),
            ],
            flops=4 * count * units * comps * width,
            nbytes=2 * units * comps * width + 4 * count * 4 * width,
            exps=count * width,
            n_in=5 + len(blocks) + len(stats),
            limit=24,
        )(
            fields,
            lin_coef,
            quad_coef,
            cross_coef.reshape(1, width),
            ply_count.reshape(1, width),
            *blocks,
            *stats,
        )
        return outs

    near_own, near_send, stat0, s0, w0 = main([near, near_twin], [f32, bf16])
    near_got = along(1, near_send)
    far_own, stat1, s1, w1 = main([far], [f32])
    far_send, stat, s2, w2 = main([far_twin], [bf16], [stat0, stat1])
    far_got = along(1, far_send)
    stat_twin = along(1, stat)

    chunk = vmem_call(
        cores_kernel,
        shape((quarter * units // 128 + 16, 128), bf16),
        flops=4 * quarter * units,
        nbytes=8 * quarter * units,
        n_in=4,
    )(far_own, far_got, stat, stat_twin)
    part = along(2, chunk)
    outs = vmem_call(
        chips_kernel,
        [shape((rows * units // 128, 128), f32), shape((1, cases), f32)]
        + [shape((rows * units // 128 + 16, 128), bf16)] * (nz - 1),
        flops=6 * quarter * units,
        nbytes=10 * quarter * units,
        n_in=5,
    )(near_own, near_got, stat, stat_twin, part)
    own, env = outs[:2]
    parts = [along(4 * m, x) for m, x in enumerate(outs[2:], start=1)]

    coef, gain = vmem_call(
        coef_kernel,
        [shape((6, width), f32), shape((rows, 128), f32)],
        flops=14 * cases * width,
        nbytes=16 * cases * width,
        n_in=9 + len(parts),
    )(cot, stat, env, s0, s1, s2, w0, w1, w2, *parts)
    bit = 1
    while bit < n_case:
        coef = coef + lax.ppermute(coef, "case", [(i, i ^ bit) for i in range(n_case)])
        bit *= 2

    load_grad = vmem_call(
        combine_kernel,
        shape((rows, units), f32),
        flops=2 * nz * rows * units,
        nbytes=2 * nz * rows * units,
        n_in=2 + len(parts),
    )(gain, own, *parts)
    return (load_grad, coef)


def solution(mesh):
    n, n_case = mesh.shape["elem"], mesh.shape["case"]
    return jax.shard_map(
        functools.partial(per_device, n, n_case),
        mesh=mesh,
        in_specs=(
            P(("case", "elem"), None),
            P(None, None, "elem"),
            P(None, None, "elem"),
            P(None, "elem"),
            P(None, "elem"),
            P("elem"),
            P("elem"),
            P("case"),
        ),
        out_specs=(P(("case", "elem"), None), P(None, "elem")),
        check_vma=False,
    )
```

```python
import functools

import jax
import jax.numpy as jnp
from jax import lax
from jax.experimental import pallas as pl
from jax.experimental.pallas import tpu as pltpu
from jax.sharding import PartitionSpec as P

JB = 256
VMEM = pltpu.VMEM


def vmem_call(kernel, out_shape, scratch_shapes=(), flops=0, nbytes=0, exps=0, n_in=0, smem=(), hbm=(), limit=16):
    def place(i):
        return pltpu.SMEM if i in smem else pltpu.HBM if i in hbm else VMEM

    return pl.pallas_call(
        kernel,
        out_shape=out_shape,
        in_specs=[pl.BlockSpec(memory_space=place(i)) for i in range(n_in)],
        out_specs=jax.tree.map(lambda _: pl.BlockSpec(memory_space=VMEM), out_shape),
        scratch_shapes=list(scratch_shapes),
        cost_estimate=pl.CostEstimate(flops=flops, bytes_accessed=nbytes, transcendentals=exps),
        compiler_params=pltpu.CompilerParams(vmem_limit_bytes=limit << 20),
    )


def to_lanes(column, rows):
    step = min(rows, 128)
    parts = []
    for at in range(0, rows, step):
        square = jnp.broadcast_to(column[at : at + step], (step, 128))
        parts.append(jnp.transpose(square)[0:1, :])
    return jnp.concatenate(parts, axis=1)


def to_rows(row, at):
    return jnp.transpose(jnp.broadcast_to(row[:, at : at + 128], (128, 128)))


def swap_lanes(x, which, width, n):
    lane = lax.broadcasted_iota(jnp.int32, x.shape, 1)
    bit = 1
    while bit < n:
        step = bit * width
        ahead = jnp.concatenate([x[:, step:], x[:, :step]], axis=1)
        behind = jnp.concatenate([x[:, -step:], x[:, :-step]], axis=1)
        other = jnp.where((lane & step) != 0, behind, ahead)
        x = jnp.where((which & bit) != 0, other, x)
        bit *= 2
    return x


def swap_halves(x):
    half = x.shape[1] // 2
    return jnp.concatenate([x[:, half:], x[:, :half]], axis=1)


def block_kernel(*refs):
    out_ref = refs[-1]
    values = [ref[...].astype(jnp.float32) for ref in refs[:-1]]
    out_ref[...] = jnp.concatenate(values, axis=0).astype(jnp.bfloat16)


def prep_kernel(n, me_ref, mant_hbm, exp_hbm, cot_ref, out_ref, turned_ref, cot_out_ref, mant, expo, sems):
    comps, units, width = mant.shape
    blocks = expo.shape[1]
    span = width // blocks
    copies = [pltpu.make_async_copy(exp_hbm, expo, sems.at[comps])]
    copies += [pltpu.make_async_copy(mant_hbm.at[k], mant.at[k], sems.at[k]) for k in range(comps)]
    for copy in copies:
        copy.start()
    cases = cot_ref.shape[1]
    rows = cases // n
    nz = n // 4
    order = [z * 4 + y * 2 + c for c in range(2) for y in range(2) for z in range(nz)]
    cot = jnp.concatenate([cot_ref[:, e * rows : (e + 1) * rows] for e in order], axis=1)
    code = (me_ref[0] & 1) * (2 * nz) + ((me_ref[0] >> 1) & 1) * nz + (me_ref[0] >> 2)
    cot = jnp.broadcast_to(cot, (8, cases))
    cot_out_ref[...] = swap_lanes(cot, jnp.full((8, cases), code, jnp.int32), rows, n)[0:1]
    copies[0].wait()
    factor = jnp.exp2(expo[...].astype(jnp.float32)).reshape(comps * blocks, units)
    pad = jnp.zeros((128 - comps * blocks, units), jnp.float32)
    columns = jnp.transpose(jnp.concatenate([factor, pad], axis=0))
    for k in range(comps):
        copies[1 + k].wait()
        for b in range(blocks):
            gain = jnp.broadcast_to(columns[:, k * blocks + b : k * blocks + b + 1], (units, span))
            value = mant[k, :, b * span : (b + 1) * span] * gain.astype(jnp.bfloat16)
            first = b * span
            at = (first // JB) * (comps * JB) + k * JB + first % JB
            out_ref[:, at : at + span] = value
            turned_ref[at : at + span, :] = jnp.transpose(value)


def main_kernel(n_rows, n_stat, f_ref, turned_ref, lin_ref, quad_ref, cross_ref, ply_ref, *refs):
    row_refs, stat_refs = refs[:n_rows], refs[n_rows : n_rows + n_stat]
    term_refs = refs[n_rows + n_stat : 2 * n_rows + n_stat]
    stat_ref, s_ref, w_ref, a_ref, idx, d, acc = refs[2 * n_rows + n_stat :]
    cases = a_ref.shape[0]
    width = w_ref.shape[1]
    at = 0
    for ref in row_refs:
        a_ref[at : at + ref.shape[0], :] = ref[...]
        at += ref.shape[0]
    tile = 32
    peak = jnp.full((cases, 128), -jnp.inf, jnp.float32)
    for jb in range(width // JB):
        cols = slice(jb * JB, (jb + 1) * JB)
        base = jb * 3 * JB
        s_ref[:, base : base + 3 * JB] = jnp.dot(
            a_ref[...], f_ref[:, base : base + 3 * JB], preferred_element_type=jnp.float32
        )
        f1, f2 = lin_ref[0:1, cols], lin_ref[1:2, cols]
        f11, f22, f66 = quad_ref[0:1, cols], quad_ref[1:2, cols], quad_ref[2:3, cols]
        f12 = 2.0 * cross_ref[0:1, cols]
        tops = []
        for at in range(0, cases, tile):
            r = slice(at, at + tile)
            s1 = s_ref[r, base : base + JB]
            s2 = s_ref[r, base + JB : base + 2 * JB]
            t = s_ref[r, base + 2 * JB : base + 3 * JB]
            index = s1 * (f1 + f11 * s1 + f12 * s2) + s2 * (f2 + f22 * s2) + f66 * (t * t)
            idx[r, cols] = index
            top = index[:, 0:128]
            for c in range(128, JB, 128):
                top = jnp.maximum(top, index[:, c : c + 128])
            tops.append(top)
        peak = jnp.maximum(peak, jnp.concatenate(tops, axis=0))
    peak = jnp.max(peak, axis=1, keepdims=True)

    total = jnp.zeros((cases, 128), jnp.float32)
    for jb in range(width // JB):
        cols = slice(jb * JB, (jb + 1) * JB)
        base = jb * 3 * JB
        f1, f2 = lin_ref[0:1, cols], lin_ref[1:2, cols]
        q11, q22, q66 = 2.0 * quad_ref[0:1, cols], 2.0 * quad_ref[1:2, cols], 2.0 * quad_ref[2:3, cols]
        f12 = 2.0 * cross_ref[0:1, cols]
        plies = (ply_ref[0:1, cols] + 1).astype(jnp.float32)
        sums = []
        for at in range(0, cases, tile):
            r = slice(at, at + tile)
            s1 = s_ref[r, base : base + JB]
            s2 = s_ref[r, base + JB : base + 2 * JB]
            t = s_ref[r, base + 2 * JB : base + 3 * JB]
            w = plies * jnp.exp(idx[r, cols] - peak[r])
            w_ref[r, cols] = w
            part = w[:, 0:128]
            for c in range(128, JB, 128):
                part = part + w[:, c : c + 128]
            sums.append(part)
            d[r, base : base + JB] = (w * (f1 + q11 * s1 + f12 * s2)).astype(jnp.bfloat16)
            d[r, base + JB : base + 2 * JB] = (w * (f2 + q22 * s2 + f12 * s1)).astype(jnp.bfloat16)
            d[r, base + 2 * JB : base + 3 * JB] = (w * (q66 * t)).astype(jnp.bfloat16)
        total = total + jnp.concatenate(sums, axis=0)
        part = jnp.dot(
            d[:, base : base + 3 * JB],
            turned_ref[base : base + 3 * JB, :],
            preferred_element_type=jnp.float32,
        )
        if jb == 0:
            acc[...] = part
        elif jb < width // JB - 1:
            acc[...] += part
        else:
            total = jnp.sum(total, axis=1, keepdims=True)
            part = (acc[...] + part) * (1.0 / total)
            at = 0
            for ref in term_refs:
                ref[...] = part[at : at + ref.shape[0]].astype(ref.dtype)
                at += ref.shape[0]
    lines = [to_lanes(peak, cases), to_lanes(peak + jnp.log(total), cases)]
    half = cases // 2
    if stat_refs:
        near = stat_refs[0]
        stat_ref[:, 0:half] = near[:, 0:half]
        stat_ref[:, 2 * half : 3 * half] = near[:, half:]
        places = [(half, 0), (3 * half, half)]
    else:
        places = [(0, 0), (half, half)]
    for here, there in places:
        for i in range(2):
            stat_ref[i : i + 1, here : here + half] = lines[i][:, there : there + half]


def join(a, b):
    top = jnp.maximum(a, b)
    return top + jnp.log(jnp.exp(a - top) + jnp.exp(b - top))


def encode(env):
    groups = env.shape[1] // 128
    lines = jnp.concatenate([env[:, g * 128 : (g + 1) * 128] for g in range(groups)], axis=0)
    high = lines.astype(jnp.bfloat16).astype(jnp.float32)
    middle = (lines - high).astype(jnp.bfloat16).astype(jnp.float32)
    rest = jnp.zeros((16 - 3 * groups, 128), jnp.float32)
    return jnp.concatenate([high, middle, lines - high - middle, rest], axis=0).astype(jnp.bfloat16)


def decode(ref, cases):
    size, groups = ref.shape[0] - 16, cases // 128
    lines = ref[size : size + 16, :].astype(jnp.float32)
    lines = lines[0:groups] + lines[groups : 2 * groups] + lines[2 * groups : 3 * groups]
    return jnp.concatenate([lines[g : g + 1] for g in range(groups)], axis=1)


def fold(x):
    return jnp.concatenate([x[:, c : c + 128] for c in range(0, x.shape[1], 128)], axis=0)


def cores_kernel(own_ref, got_ref, stat_ref, twin_ref, out_ref):
    quarter = own_ref.shape[0]
    cases = 4 * quarter
    mine, theirs = stat_ref[1:2, :], swap_halves(twin_ref[1:2, :])
    env = join(mine, theirs)
    r = slice(quarter, 2 * quarter)
    up = column(jnp.exp(mine - env)[:, r], quarter)
    down = column(jnp.exp(theirs - env)[:, r], quarter)
    value = own_ref[...] * up + got_ref[...] * down
    size = out_ref.shape[0] - 16
    out_ref[0:size, :] = fold(value).astype(jnp.bfloat16)
    out_ref[size : size + 16, :] = encode(env)


def column(row, rows):
    return jnp.concatenate([to_rows(row, at)[:, 0:1] for at in range(0, rows, 128)], axis=0)


def chips_kernel(own_ref, got_ref, stat_ref, twin_ref, part_ref, own_out_ref, env_ref, *out_refs):
    quarter, units = own_ref.shape
    cases = 4 * quarter
    rows = quarter // (1 + len(out_refs))
    mine, theirs = stat_ref[1:2, :], swap_halves(twin_ref[1:2, :])
    far = decode(part_ref, cases)
    far = jnp.concatenate([far[:, g * quarter : (g + 1) * quarter] for g in (1, 0, 3, 2)], axis=1)
    env = join(join(mine, theirs), far)
    env_ref[...] = env
    scale = [column(jnp.exp(x - env)[:, 0:quarter], quarter) for x in (mine, theirs, far)]
    total = own_ref[...] * scale[0] + got_ref[...] * scale[1]
    parts = []
    for c in range(units // 128):
        part = part_ref[c * quarter : (c + 1) * quarter, :].astype(jnp.float32)
        parts.append(total[:, c * 128 : (c + 1) * 128] + part * scale[2])
    own_out_ref[...] = jnp.concatenate([p[0:rows] for p in parts], axis=0)
    tail = encode(env)
    for m, ref in enumerate(out_refs):
        r = slice((m + 1) * rows, (m + 2) * rows)
        size = ref.shape[0] - 16
        ref[0:size, :] = jnp.concatenate([p[r] for p in parts], axis=0).astype(jnp.bfloat16)
        ref[size : size + 16, :] = tail


def coef_kernel(cot_ref, stat_ref, env_ref, s0_ref, s1_ref, w0_ref, w1_ref, *refs):
    coef_ref, gain_ref = refs[-2:]
    part_refs = refs[:-2]
    nz = 1 + len(part_refs)
    cases = cot_ref.shape[1]
    quarter = cases // 4
    rows = quarter // nz
    width = w0_ref.shape[1]
    envs = [env_ref[...]] + [decode(ref, cases) for ref in part_refs]
    pad = -nz % 8
    env_all = jnp.concatenate(envs + [envs[0]] * pad, axis=0)
    which = lax.broadcasted_iota(jnp.int32, env_all.shape, 0)
    env_all = swap_lanes(env_all, jnp.where(which < nz, which, 0), rows, nz)[0:nz]
    top = jnp.max(env_all, axis=0, keepdims=True)
    env = top + jnp.log(jnp.sum(jnp.exp(env_all - top), axis=0, keepdims=True))
    cot = cot_ref[...]
    gain = cot[:, 0:128] * jnp.exp(env_all[:, 0:128] - env[:, 0:128])
    fill = jnp.zeros((128 - nz, 128), jnp.float32)
    gain_ref[...] = jnp.transpose(jnp.concatenate([gain, fill], axis=0))[0:rows]
    scale = cot * jnp.exp(stat_ref[0:1, :] - env)
    scales = [to_rows(scale, at) for at in range(0, cases, 128)]
    sets = [
        (0, s0_ref, w0_ref, 0),
        (quarter, s1_ref, w1_ref, 0),
        (2 * quarter, s0_ref, w0_ref, quarter),
        (3 * quarter, s1_ref, w1_ref, quarter),
    ]
    for jb in range(width // JB):
        base = jb * 3 * JB
        for c in range(0, JB, 128):
            sums = [jnp.zeros((8, 128), jnp.float32) for _ in range(6)]
            for here, s_ref, w_ref, there in sets:
                for at in range(0, quarter, 8):
                    r = slice(there + at, there + at + 8)
                    s1 = s_ref[r, base + c : base + c + 128]
                    s2 = s_ref[r, base + JB + c : base + JB + c + 128]
                    t = s_ref[r, base + 2 * JB + c : base + 2 * JB + c + 128]
                    place = here + at
                    gain = scales[place // 128][place % 128 : place % 128 + 8]
                    w = w_ref[r, jb * JB + c : jb * JB + c + 128] * gain
                    a, b = w * s1, w * s2
                    for i, v in enumerate((a, b, a * s1, b * s2, w * t * t, a * s2)):
                        sums[i] = sums[i] + v
            for i in range(6):
                line = jnp.sum(sums[i], axis=0, keepdims=True)
                if i == 5:
                    line = 2.0 * line
                coef_ref[i : i + 1, jb * JB + c : jb * JB + c + 128] = line


def combine_kernel(gain_ref, own_ref, *refs):
    part_refs, out_ref = refs[:-1], refs[-1]
    rows, units = out_ref.shape
    size = rows * units // 128
    for c in range(units // 128):
        r = slice(c * rows, (c + 1) * rows)
        value = own_ref[r, :] * gain_ref[:, 0:1]
        for m, ref in enumerate(part_refs):
            part = ref[0:size, :].astype(jnp.float32)[r]
            value = value + part * gain_ref[:, m + 1 : m + 2]
        out_ref[:, c * 128 : (c + 1) * 128] = value


def per_device(n, n_case, load_coef, mantissa, scale_exp, lin_coef, quad_coef, cross_coef, ply_count, cotangent):
    units, comps, width = mantissa.shape
    rows = load_coef.shape[0]
    cases = rows * n
    nz = n // 4
    quarter = rows * nz
    f32, bf16 = jnp.float32, jnp.bfloat16
    shape = jax.ShapeDtypeStruct
    me = lax.axis_index("elem").astype(jnp.int32).reshape(1)

    def along(bits, x):
        return lax.ppermute(x, "elem", [(i, i ^ bits) for i in range(n)])

    along_z = [along(4 * m, load_coef) for m in range(1, nz)]
    fields, turned, cot = vmem_call(
        functools.partial(prep_kernel, n),
        [shape((units, comps * width), bf16), shape((comps * width, units), bf16), shape((1, cases), f32)],
        scratch_shapes=[
            VMEM((comps, units, width), bf16),
            VMEM((comps, scale_exp.shape[2], units), jnp.int32),
            pltpu.SemaphoreType.DMA((comps + 1,)),
        ],
        flops=units * comps * width,
        nbytes=4 * units * comps * width,
        n_in=4,
        smem=(0,),
        hbm=(1, 2),
    )(
        me,
        pltpu.with_memory_space_constraint(jnp.transpose(mantissa, (1, 0, 2)), pltpu.HBM),
        pltpu.with_memory_space_constraint(jnp.transpose(scale_exp, (1, 2, 0)), pltpu.HBM),
        cotangent.reshape(1, cases),
    )
    along_z[0], fields = lax.optimization_barrier((along_z[0], fields))
    near = vmem_call(block_kernel, shape((quarter, units), bf16), nbytes=4 * quarter * units, n_in=nz)(
        load_coef, *along_z
    )
    far = along(2, near)
    near_twin = along(1, near)

    def main(blocks, dtypes, stats=()):
        count = len(blocks) * quarter
        outs = vmem_call(
            functools.partial(main_kernel, len(blocks), len(stats)),
            [shape((quarter, units), dtype) for dtype in dtypes]
            + [
                shape((2, cases if stats else count), f32),
                shape((count, comps * width), f32),
                shape((count, width), f32),
            ],
            scratch_shapes=[
                VMEM((count, units), bf16),
                VMEM((count, width), f32),
                VMEM((count, comps * width), bf16),
                VMEM((count, units), f32),
            ],
            flops=4 * count * units * comps * width,
            nbytes=2 * units * comps * width + 4 * count * 4 * width,
            exps=count * width,
            n_in=6 + len(blocks) + len(stats),
            limit=24,
        )(
            fields,
            turned,
            lin_coef,
            quad_coef,
            cross_coef.reshape(1, width),
            ply_count.reshape(1, width),
            *blocks,
            *stats,
        )
        return outs

    near_own, near_send, near_stat, s0, w0 = main([near, near_twin], [f32, f32])
    far, near_send = lax.optimization_barrier((far, near_send))
    near_got = along(1, near_send)
    far_own, far_send, stat, s1, w1 = main([far, along(1, far)], [f32, f32], [near_stat])
    far_got, stat_twin = along(1, far_send), along(1, stat)

    chunk = vmem_call(
        cores_kernel,
        shape((quarter * units // 128 + 16, 128), bf16),
        flops=4 * quarter * units,
        nbytes=8 * quarter * units,
        n_in=4,
    )(far_own, far_got, stat, stat_twin)
    part = along(2, chunk)
    outs = vmem_call(
        chips_kernel,
        [shape((rows * units // 128, 128), f32), shape((1, cases), f32)]
        + [shape((rows * units // 128 + 16, 128), bf16)] * (nz - 1),
        flops=6 * quarter * units,
        nbytes=10 * quarter * units,
        n_in=5,
    )(near_own, near_got, stat, stat_twin, part)
    own, env = outs[:2]
    parts = [along(4 * m, x) for m, x in enumerate(outs[2:], start=1)]

    coef, gain = vmem_call(
        coef_kernel,
        [shape((6, width), f32), shape((rows, 128), f32)],
        flops=14 * cases * width,
        nbytes=16 * cases * width,
        n_in=7 + len(parts),
    )(cot, stat, env, s0, s1, w0, w1, *parts)
    bit = 1
    while bit < n_case:
        coef = coef + lax.ppermute(coef, "case", [(i, i ^ bit) for i in range(n_case)])
        bit *= 2

    load_grad = vmem_call(
        combine_kernel,
        shape((rows, units), f32),
        flops=2 * nz * rows * units,
        nbytes=2 * nz * rows * units,
        n_in=2 + len(parts),
    )(gain, own, *parts)
    return (load_grad, coef)


def solution(mesh):
    n, n_case = mesh.shape["elem"], mesh.shape["case"]
    return jax.shard_map(
        functools.partial(per_device, n, n_case),
        mesh=mesh,
        in_specs=(
            P(("case", "elem"), None),
            P(None, None, "elem"),
            P(None, None, "elem"),
            P(None, "elem"),
            P(None, "elem"),
            P("elem"),
            P("elem"),
            P("case"),
        ),
        out_specs=(P(("case", "elem"), None), P(None, "elem")),
        check_vma=False,
    )
```

```python
import functools

import jax
import jax.numpy as jnp
from jax import lax
from jax.experimental import pallas as pl
from jax.experimental.pallas import tpu as pltpu
from jax.sharding import PartitionSpec as P

JB = 256
VMEM = pltpu.VMEM


def vmem_call(kernel, out_shape, scratch_shapes=(), flops=0, nbytes=0, exps=0, n_in=0, smem=(), hbm=(), limit=16):
    def place(i):
        return pltpu.SMEM if i in smem else pltpu.HBM if i in hbm else VMEM

    return pl.pallas_call(
        kernel,
        out_shape=out_shape,
        in_specs=[pl.BlockSpec(memory_space=place(i)) for i in range(n_in)],
        out_specs=jax.tree.map(lambda _: pl.BlockSpec(memory_space=VMEM), out_shape),
        scratch_shapes=list(scratch_shapes),
        cost_estimate=pl.CostEstimate(flops=flops, bytes_accessed=nbytes, transcendentals=exps),
        compiler_params=pltpu.CompilerParams(vmem_limit_bytes=limit << 20),
    )


def to_lanes(column, rows):
    step = min(rows, 128)
    parts = []
    for at in range(0, rows, step):
        square = jnp.broadcast_to(column[at : at + step], (step, 128))
        parts.append(jnp.transpose(square)[0:1, :])
    return jnp.concatenate(parts, axis=1)


def to_rows(row, at):
    return jnp.transpose(jnp.broadcast_to(row[:, at : at + 128], (128, 128)))


def swap_lanes(x, which, width, n):
    lane = lax.broadcasted_iota(jnp.int32, x.shape, 1)
    bit = 1
    while bit < n:
        step = bit * width
        ahead = jnp.concatenate([x[:, step:], x[:, :step]], axis=1)
        behind = jnp.concatenate([x[:, -step:], x[:, :-step]], axis=1)
        other = jnp.where((lane & step) != 0, behind, ahead)
        x = jnp.where((which & bit) != 0, other, x)
        bit *= 2
    return x


def swap_halves(x):
    half = x.shape[1] // 2
    return jnp.concatenate([x[:, half:], x[:, :half]], axis=1)


def block_kernel(*refs):
    out_ref = refs[-1]
    values = [ref[...].astype(jnp.float32) for ref in refs[-2::-1]]
    out_ref[...] = jnp.concatenate(values, axis=0).astype(jnp.bfloat16)


def prep_kernel(n, me_ref, mant_hbm, exp_hbm, cot_hbm, out_ref, cot_out_ref, mant, expo, cot_ref, sems):
    comps, units, width = mant.shape
    blocks = expo.shape[1]
    span = width // blocks
    copies = [
        pltpu.make_async_copy(cot_hbm, cot_ref, sems.at[comps + 1]),
        pltpu.make_async_copy(exp_hbm, expo, sems.at[comps]),
    ]
    copies += [pltpu.make_async_copy(mant_hbm.at[k], mant.at[k], sems.at[k]) for k in range(comps)]
    for copy in copies:
        copy.start()
    copies[0].wait()
    cases = cot_ref.shape[1]
    rows = cases // n
    nz = n // 4
    order = [z * 4 + y * 2 + c for c in range(2) for y in range(2) for z in range(nz)]
    cot = jnp.concatenate([cot_ref[:, e * rows : (e + 1) * rows] for e in order], axis=1)
    code = (me_ref[0] & 1) * (2 * nz) + ((me_ref[0] >> 1) & 1) * nz + (me_ref[0] >> 2)
    cot = jnp.broadcast_to(cot, (8, cases))
    cot_out_ref[...] = swap_lanes(cot, jnp.full((8, cases), code, jnp.int32), rows, n)[0:1]
    copies[1].wait()
    factor = jnp.exp2(expo[...].astype(jnp.float32)).reshape(comps * blocks, units)
    pad = jnp.zeros((128 - comps * blocks, units), jnp.float32)
    columns = jnp.transpose(jnp.concatenate([factor, pad], axis=0))
    for k in range(comps):
        copies[2 + k].wait()
        for b in range(blocks):
            gain = jnp.broadcast_to(columns[:, k * blocks + b : k * blocks + b + 1], (units, span))
            value = mant[k, :, b * span : (b + 1) * span] * gain.astype(jnp.bfloat16)
            first = b * span
            at = (first // JB) * (comps * JB) + k * JB + first % JB
            out_ref[:, at : at + span] = value


def main_kernel(n_rows, n_stat, f_ref, lin_ref, quad_ref, cross_ref, ply_ref, *refs):
    row_refs, stat_refs = refs[:n_rows], refs[n_rows : n_rows + n_stat]
    term_refs = refs[n_rows + n_stat : 2 * n_rows + n_stat]
    stat_ref, s_ref, w_ref, a_ref, idx, d, rest, acc = refs[2 * n_rows + n_stat :]
    cases = a_ref.shape[0]
    width = w_ref.shape[1]
    at = 0
    for ref in row_refs:
        a_ref[at : at + ref.shape[0], :] = ref[...]
        at += ref.shape[0]
    tile = 32
    peak = jnp.full((cases, 128), -jnp.inf, jnp.float32)
    for jb in range(width // JB):
        cols = slice(jb * JB, (jb + 1) * JB)
        base = jb * 3 * JB
        s_ref[:, base : base + 3 * JB] = jnp.dot(
            a_ref[...], f_ref[:, base : base + 3 * JB], preferred_element_type=jnp.float32
        )
        f1, f2 = lin_ref[0:1, cols], lin_ref[1:2, cols]
        f11, f22, f66 = quad_ref[0:1, cols], quad_ref[1:2, cols], quad_ref[2:3, cols]
        f12 = 2.0 * cross_ref[0:1, cols]
        tops = []
        for at in range(0, cases, tile):
            r = slice(at, at + tile)
            s1 = s_ref[r, base : base + JB]
            s2 = s_ref[r, base + JB : base + 2 * JB]
            t = s_ref[r, base + 2 * JB : base + 3 * JB]
            index = s1 * (f1 + f11 * s1 + f12 * s2) + s2 * (f2 + f22 * s2) + f66 * (t * t)
            idx[r, cols] = index
            top = index[:, 0:128]
            for c in range(128, JB, 128):
                top = jnp.maximum(top, index[:, c : c + 128])
            tops.append(top)
        peak = jnp.maximum(peak, jnp.concatenate(tops, axis=0))
    peak = jnp.max(peak, axis=1, keepdims=True)

    total = jnp.zeros((cases, 128), jnp.float32)
    for jb in range(width // JB):
        cols = slice(jb * JB, (jb + 1) * JB)
        base = jb * 3 * JB
        f1, f2 = lin_ref[0:1, cols], lin_ref[1:2, cols]
        q11, q22, q66 = 2.0 * quad_ref[0:1, cols], 2.0 * quad_ref[1:2, cols], 2.0 * quad_ref[2:3, cols]
        f12 = 2.0 * cross_ref[0:1, cols]
        plies = (ply_ref[0:1, cols] + 1).astype(jnp.float32)
        sums = []
        for at in range(0, cases, tile):
            r = slice(at, at + tile)
            s1 = s_ref[r, base : base + JB]
            s2 = s_ref[r, base + JB : base + 2 * JB]
            t = s_ref[r, base + 2 * JB : base + 3 * JB]
            w = plies * jnp.exp(idx[r, cols] - peak[r])
            w_ref[r, cols] = w
            part = w[:, 0:128]
            for c in range(128, JB, 128):
                part = part + w[:, c : c + 128]
            sums.append(part)
            for k, slope in enumerate((f1 + q11 * s1 + f12 * s2, f2 + q22 * s2 + f12 * s1, q66 * t)):
                value = w * slope
                high = value.astype(jnp.bfloat16)
                at_k = slice(base + k * JB, base + (k + 1) * JB)
                d[r, at_k] = high
                rest[r, at_k] = (value - high.astype(jnp.float32)).astype(jnp.bfloat16)
        total = total + jnp.concatenate(sums, axis=0)
        part = 0.0
        for term in (d, rest):
            part = part + lax.dot_general(
                term[:, base : base + 3 * JB],
                f_ref[:, base : base + 3 * JB],
                (((1,), (1,)), ((), ())),
                preferred_element_type=jnp.float32,
            )
        if jb == 0:
            acc[...] = part
        elif jb < width // JB - 1:
            acc[...] += part
        else:
            total = jnp.sum(total, axis=1, keepdims=True)
            part = (acc[...] + part) * (1.0 / total)
            at = 0
            for ref in term_refs:
                ref[...] = part[at : at + ref.shape[0]].astype(ref.dtype)
                at += ref.shape[0]
    lines = [to_lanes(peak, cases), to_lanes(peak + jnp.log(total), cases)]
    half = cases // 2
    if stat_refs:
        near = stat_refs[0]
        stat_ref[:, 0:half] = near[:, 0:half]
        stat_ref[:, 2 * half : 3 * half] = near[:, half:]
        places = [(half, 0), (3 * half, half)]
    else:
        places = [(0, 0), (half, half)]
    for here, there in places:
        for i in range(2):
            stat_ref[i : i + 1, here : here + half] = lines[i][:, there : there + half]


def join(a, b):
    top = jnp.maximum(a, b)
    return top + jnp.log(jnp.exp(a - top) + jnp.exp(b - top))


def encode(env):
    groups = env.shape[1] // 128
    lines = jnp.concatenate([env[:, g * 128 : (g + 1) * 128] for g in range(groups)], axis=0)
    high = lines.astype(jnp.bfloat16).astype(jnp.float32)
    middle = (lines - high).astype(jnp.bfloat16).astype(jnp.float32)
    rest = jnp.zeros((16 - 3 * groups, 128), jnp.float32)
    return jnp.concatenate([high, middle, lines - high - middle, rest], axis=0).astype(jnp.bfloat16)


def decode(ref, cases):
    size, groups = ref.shape[0] - 16, cases // 128
    lines = ref[size : size + 16, :].astype(jnp.float32)
    lines = lines[0:groups] + lines[groups : 2 * groups] + lines[2 * groups : 3 * groups]
    return jnp.concatenate([lines[g : g + 1] for g in range(groups)], axis=1)


def fold(x):
    return jnp.concatenate([x[:, c : c + 128] for c in range(0, x.shape[1], 128)], axis=0)


def cores_kernel(own_ref, got_ref, stat_ref, twin_ref, out_ref, env_ref):
    quarter = own_ref.shape[0]
    cases = 4 * quarter
    mine, theirs = stat_ref[1:2, :], swap_halves(twin_ref[1:2, :])
    env = join(mine, theirs)
    env_ref[...] = env
    r = slice(quarter, 2 * quarter)
    up = column(jnp.exp(mine - env)[:, r], quarter)
    down = column(jnp.exp(theirs - env)[:, r], quarter)
    value = own_ref[...] * up + got_ref[...] * down
    size = out_ref.shape[0] - 16
    out_ref[0:size, :] = fold(value).astype(jnp.bfloat16)
    out_ref[size : size + 16, :] = encode(env)


def column(row, rows):
    return jnp.concatenate([to_rows(row, at)[:, 0:1] for at in range(0, rows, 128)], axis=0)


def chips_kernel(nz, own_ref, got_ref, stat_ref, twin_ref, part_ref, *refs):
    env_refs, stack_ref, own_out_ref, out_refs = refs[:nz], refs[nz], refs[nz + 1], refs[nz + 2 :]
    quarter = own_ref.shape[0]
    units = own_ref.shape[1]
    cases = 4 * quarter
    rows = quarter // nz
    stack_ref[...] = jnp.concatenate([ref[...] for ref in env_refs], axis=0)
    mine, theirs = stat_ref[1:2, :], swap_halves(twin_ref[1:2, :])
    far = decode(part_ref, cases)
    far = jnp.concatenate([far[:, g * quarter : (g + 1) * quarter] for g in (1, 0, 3, 2)], axis=1)
    env = join(join(mine, theirs), far)
    scale = [column(jnp.exp(x - env)[:, 0:quarter], quarter) for x in (mine, theirs, far)]
    total = own_ref[...] * scale[0] + got_ref[...] * scale[1]
    parts = []
    for c in range(units // 128):
        part = part_ref[c * quarter : (c + 1) * quarter, :].astype(jnp.float32)
        parts.append(total[:, c * 128 : (c + 1) * 128] + part * scale[2])
    own_out_ref[...] = jnp.concatenate([p[0:rows] for p in parts], axis=0)
    for m, ref in enumerate(out_refs):
        r = slice((m + 1) * rows, (m + 2) * rows)
        ref[...] = jnp.concatenate([p[r] for p in parts], axis=0).astype(jnp.bfloat16)


def coef_kernel(cot_ref, stat_ref, near_ref, far_ref, s0_ref, s1_ref, w0_ref, w1_ref, coef_ref, gain_ref):
    nz, cases = near_ref.shape
    quarter = cases // 4
    rows = quarter // nz
    width = w0_ref.shape[1]
    row = lax.broadcasted_iota(jnp.int32, (nz, cases), 0)
    near = swap_lanes(near_ref[...], row, rows, 2 * nz)
    far = swap_lanes(far_ref[...], row + nz, rows, 2 * nz)
    env_all = join(near, far)
    top = jnp.max(env_all, axis=0, keepdims=True)
    env = top + jnp.log(jnp.sum(jnp.exp(env_all - top), axis=0, keepdims=True))
    cot = cot_ref[...]
    gain = cot[:, 0:128] * jnp.exp(env_all[:, 0:128] - env[:, 0:128])
    fill = jnp.zeros((128 - nz, 128), jnp.float32)
    gain_ref[...] = jnp.transpose(jnp.concatenate([gain, fill], axis=0))[0:rows]
    scale = cot * jnp.exp(stat_ref[0:1, :] - env)
    scales = [to_rows(scale, at) for at in range(0, cases, 128)]
    sets = [
        (0, s0_ref, w0_ref, 0),
        (quarter, s1_ref, w1_ref, 0),
        (2 * quarter, s0_ref, w0_ref, quarter),
        (3 * quarter, s1_ref, w1_ref, quarter),
    ]
    for jb in range(width // JB):
        base = jb * 3 * JB
        for c in range(0, JB, 128):
            sums = [jnp.zeros((8, 128), jnp.float32) for _ in range(6)]
            for here, s_ref, w_ref, there in sets:
                for at in range(0, quarter, 8):
                    r = slice(there + at, there + at + 8)
                    s1 = s_ref[r, base + c : base + c + 128]
                    s2 = s_ref[r, base + JB + c : base + JB + c + 128]
                    t = s_ref[r, base + 2 * JB + c : base + 2 * JB + c + 128]
                    place = here + at
                    gain = scales[place // 128][place % 128 : place % 128 + 8]
                    w = w_ref[r, jb * JB + c : jb * JB + c + 128] * gain
                    a, b = w * s1, w * s2
                    for i, v in enumerate((a, b, a * s1, b * s2, w * t * t, a * s2)):
                        sums[i] = sums[i] + v
            for i in range(6):
                line = jnp.sum(sums[i], axis=0, keepdims=True)
                if i == 5:
                    line = 2.0 * line
                coef_ref[i : i + 1, jb * JB + c : jb * JB + c + 128] = line


def combine_kernel(gain_ref, own_ref, *refs):
    part_refs, out_ref = refs[-2::-1], refs[-1]
    rows, units = out_ref.shape
    for c in range(units // 128):
        r = slice(c * rows, (c + 1) * rows)
        value = own_ref[r, :] * gain_ref[:, 0:1]
        for m, ref in enumerate(part_refs):
            part = ref[...].astype(jnp.float32)[r]
            value = value + part * gain_ref[:, m + 1 : m + 2]
        out_ref[:, c * 128 : (c + 1) * 128] = value


def per_device(n, n_case, load_coef, mantissa, scale_exp, lin_coef, quad_coef, cross_coef, ply_count, cotangent):
    units, comps, width = mantissa.shape
    rows = load_coef.shape[0]
    cases = rows * n
    nz = n // 4
    quarter = rows * nz
    f32, bf16 = jnp.float32, jnp.bfloat16
    shape = jax.ShapeDtypeStruct
    me = lax.axis_index("elem").astype(jnp.int32).reshape(1)

    def along(bits, x):
        return lax.ppermute(x, "elem", [(i, i ^ bits) for i in range(n)])

    along_z = [along(4 * m, load_coef) for m in range(nz - 1, 0, -1)]
    fields, cot = vmem_call(
        functools.partial(prep_kernel, n),
        [shape((units, comps * width), bf16), shape((1, cases), f32)],
        scratch_shapes=[
            VMEM((comps, units, width), bf16),
            VMEM((comps, scale_exp.shape[2], units), jnp.int32),
            VMEM((1, cases), f32),
            pltpu.SemaphoreType.DMA((comps + 2,)),
        ],
        flops=units * comps * width,
        nbytes=4 * units * comps * width,
        n_in=4,
        smem=(0,),
        hbm=(1, 2, 3),
    )(
        me,
        pltpu.with_memory_space_constraint(jnp.transpose(mantissa, (1, 0, 2)), pltpu.HBM),
        pltpu.with_memory_space_constraint(jnp.transpose(scale_exp, (1, 2, 0)), pltpu.HBM),
        pltpu.with_memory_space_constraint(cotangent.reshape(1, cases), pltpu.HBM),
    )
    along_z[0], fields = lax.optimization_barrier((along_z[0], fields))
    near = vmem_call(block_kernel, shape((quarter, units), bf16), nbytes=4 * quarter * units, n_in=nz)(
        *along_z, load_coef
    )
    far = along(2, near)
    near_twin = along(1, near)

    def main(blocks, dtypes, stats=()):
        count = len(blocks) * quarter
        outs = vmem_call(
            functools.partial(main_kernel, len(blocks), len(stats)),
            [shape((quarter, units), dtype) for dtype in dtypes]
            + [
                shape((2, cases if stats else count), f32),
                shape((count, comps * width), f32),
                shape((count, width), f32),
            ],
            scratch_shapes=[
                VMEM((count, units), bf16),
                VMEM((count, width), f32),
                VMEM((count, comps * width), bf16),
                VMEM((count, comps * width), bf16),
                VMEM((count, units), f32),
            ],
            flops=6 * count * units * comps * width,
            nbytes=2 * units * comps * width + 4 * count * 4 * width,
            exps=count * width,
            n_in=5 + len(blocks) + len(stats),
            limit=24,
        )(
            fields,
            lin_coef,
            quad_coef,
            cross_coef.reshape(1, width),
            ply_count.reshape(1, width),
            *blocks,
            *stats,
        )
        return outs

    near_own, near_send, near_stat, s0, w0 = main([near, near_twin], [f32, f32])
    far, near_send = lax.optimization_barrier((far, near_send))
    far_own, far_send, stat, s1, w1 = main([far, along(1, far)], [f32, f32], [near_stat])
    far_got, stat_twin = along(1, far_send), along(1, stat)

    chunk, env = vmem_call(
        cores_kernel,
        [shape((quarter * units // 128 + 16, 128), bf16), shape((1, cases), f32)],
        flops=4 * quarter * units,
        nbytes=8 * quarter * units,
        n_in=4,
    )(far_own, far_got, stat, stat_twin)
    chunk, near_send = lax.optimization_barrier((chunk, near_send))
    part, near_got = along(2, chunk), along(1, near_send)
    envs = [along(4 * m, env) for m in range(nz - 1, 0, -1)]
    outs = vmem_call(
        functools.partial(chips_kernel, nz),
        [shape((nz, cases), f32), shape((rows * units // 128, 128), f32)]
        + [shape((rows * units // 128, 128), bf16)] * (nz - 1),
        flops=6 * quarter * units,
        nbytes=10 * quarter * units,
        n_in=5 + nz,
    )(near_own, near_got, stat, stat_twin, part, env, *envs[::-1])
    stack, own = outs[:2]
    stack_far = along(2, stack)
    parts = [along(4 * m, outs[1 + m]) for m in range(nz - 1, 0, -1)]

    coef, gain = vmem_call(
        coef_kernel,
        [shape((6, width), f32), shape((rows, 128), f32)],
        flops=14 * cases * width,
        nbytes=16 * cases * width,
        n_in=8,
    )(cot, stat, stack, stack_far, s0, s1, w0, w1)
    bit = 1
    while bit < n_case:
        coef = coef + lax.ppermute(coef, "case", [(i, i ^ bit) for i in range(n_case)])
        bit *= 2

    load_grad = vmem_call(
        combine_kernel,
        shape((rows, units), f32),
        flops=2 * nz * rows * units,
        nbytes=2 * nz * rows * units,
        n_in=2 + len(parts),
    )(gain, own, *parts)
    return (load_grad, coef)


def solution(mesh):
    n, n_case = mesh.shape["elem"], mesh.shape["case"]
    return jax.shard_map(
        functools.partial(per_device, n, n_case),
        mesh=mesh,
        in_specs=(
            P(("case", "elem"), None),
            P(None, None, "elem"),
            P(None, None, "elem"),
            P(None, "elem"),
            P(None, "elem"),
            P("elem"),
            P("elem"),
            P("case"),
        ),
        out_specs=(P(("case", "elem"), None), P(None, "elem")),
        check_vma=False,
    )
```

```python
import functools

import jax
import jax.numpy as jnp
from jax import lax
from jax.experimental import pallas as pl
from jax.experimental.pallas import tpu as pltpu
from jax.sharding import PartitionSpec as P

JB = 256
VMEM = pltpu.VMEM


def vmem_call(kernel, out_shape, scratch_shapes=(), flops=0, nbytes=0, exps=0, n_in=0, smem=(), hbm=(), limit=16):
    def place(i):
        return pltpu.SMEM if i in smem else pltpu.HBM if i in hbm else VMEM

    return pl.pallas_call(
        kernel,
        out_shape=out_shape,
        in_specs=[pl.BlockSpec(memory_space=place(i)) for i in range(n_in)],
        out_specs=jax.tree.map(lambda _: pl.BlockSpec(memory_space=VMEM), out_shape),
        scratch_shapes=list(scratch_shapes),
        cost_estimate=pl.CostEstimate(flops=flops, bytes_accessed=nbytes, transcendentals=exps),
        compiler_params=pltpu.CompilerParams(vmem_limit_bytes=limit << 20),
    )


def to_lanes(column, rows):
    step = min(rows, 128)
    parts = []
    for at in range(0, rows, step):
        square = jnp.broadcast_to(column[at : at + step], (step, 128))
        parts.append(jnp.transpose(square)[0:1, :])
    return jnp.concatenate(parts, axis=1)


def to_rows(row, at):
    return jnp.transpose(jnp.broadcast_to(row[:, at : at + 128], (128, 128)))


def swap_lanes(x, which, width, n):
    lane = lax.broadcasted_iota(jnp.int32, x.shape, 1)
    bit = 1
    while bit < n:
        step = bit * width
        ahead = jnp.concatenate([x[:, step:], x[:, :step]], axis=1)
        behind = jnp.concatenate([x[:, -step:], x[:, :-step]], axis=1)
        other = jnp.where((lane & step) != 0, behind, ahead)
        x = jnp.where((which & bit) != 0, other, x)
        bit *= 2
    return x


def swap_halves(x):
    half = x.shape[1] // 2
    return jnp.concatenate([x[:, half:], x[:, :half]], axis=1)


def block_kernel(*refs):
    out_ref = refs[-1]
    values = [ref[...].astype(jnp.float32) for ref in refs[-2::-1]]
    out_ref[...] = jnp.concatenate(values, axis=0).astype(jnp.bfloat16)


def prep_kernel(n, me_ref, mant_hbm, exp_hbm, cot_hbm, out_ref, cot_out_ref, mant, expo, cot_ref, sems):
    comps, units, width = mant.shape
    blocks = expo.shape[1]
    span = width // blocks
    copies = [
        pltpu.make_async_copy(cot_hbm, cot_ref, sems.at[comps + 1]),
        pltpu.make_async_copy(exp_hbm, expo, sems.at[comps]),
    ]
    copies += [pltpu.make_async_copy(mant_hbm.at[k], mant.at[k], sems.at[k]) for k in range(comps)]
    for copy in copies:
        copy.start()
    copies[0].wait()
    cases = cot_ref.shape[1]
    rows = cases // n
    nz = n // 4
    order = [z * 4 + y * 2 + c for c in range(2) for y in range(2) for z in range(nz)]
    cot = jnp.concatenate([cot_ref[:, e * rows : (e + 1) * rows] for e in order], axis=1)
    code = (me_ref[0] & 1) * (2 * nz) + ((me_ref[0] >> 1) & 1) * nz + (me_ref[0] >> 2)
    cot = jnp.broadcast_to(cot, (8, cases))
    cot_out_ref[...] = swap_lanes(cot, jnp.full((8, cases), code, jnp.int32), rows, n)[0:1]
    copies[1].wait()
    factor = jnp.exp2(expo[...].astype(jnp.float32)).reshape(comps * blocks, units)
    pad = jnp.zeros((128 - comps * blocks, units), jnp.float32)
    columns = jnp.transpose(jnp.concatenate([factor, pad], axis=0))
    for k in range(comps):
        copies[2 + k].wait()
        for b in range(blocks):
            gain = jnp.broadcast_to(columns[:, k * blocks + b : k * blocks + b + 1], (units, span))
            value = mant[k, :, b * span : (b + 1) * span] * gain.astype(jnp.bfloat16)
            first = b * span
            at = (first // JB) * (comps * JB) + k * JB + first % JB
            out_ref[:, at : at + span] = value


def main_kernel(n_rows, n_stat, f_ref, lin_ref, quad_ref, cross_ref, ply_ref, *refs):
    row_refs, stat_refs = refs[:n_rows], refs[n_rows : n_rows + n_stat]
    term_refs = refs[n_rows + n_stat : 2 * n_rows + n_stat]
    stat_ref, s_ref, w_ref, a_ref, idx, d, rest, acc = refs[2 * n_rows + n_stat :]
    cases = a_ref.shape[0]
    width = w_ref.shape[1]
    at = 0
    for ref in row_refs:
        a_ref[at : at + ref.shape[0], :] = ref[...]
        at += ref.shape[0]
    tile = 32
    peak = jnp.full((cases, 128), -jnp.inf, jnp.float32)
    for jb in range(width // JB):
        cols = slice(jb * JB, (jb + 1) * JB)
        base = jb * 3 * JB
        s_ref[:, base : base + 3 * JB] = jnp.dot(
            a_ref[...], f_ref[:, base : base + 3 * JB], preferred_element_type=jnp.float32
        )
        f1, f2 = lin_ref[0:1, cols], lin_ref[1:2, cols]
        f11, f22, f66 = quad_ref[0:1, cols], quad_ref[1:2, cols], quad_ref[2:3, cols]
        f12 = 2.0 * cross_ref[0:1, cols]
        tops = []
        for at in range(0, cases, tile):
            r = slice(at, at + tile)
            s1 = s_ref[r, base : base + JB]
            s2 = s_ref[r, base + JB : base + 2 * JB]
            t = s_ref[r, base + 2 * JB : base + 3 * JB]
            index = s1 * (f1 + f11 * s1 + f12 * s2) + s2 * (f2 + f22 * s2) + f66 * (t * t)
            idx[r, cols] = index
            top = index[:, 0:128]
            for c in range(128, JB, 128):
                top = jnp.maximum(top, index[:, c : c + 128])
            tops.append(top)
        peak = jnp.maximum(peak, jnp.concatenate(tops, axis=0))
    peak = jnp.max(peak, axis=1, keepdims=True)

    total = jnp.zeros((cases, 128), jnp.float32)
    for jb in range(width // JB):
        cols = slice(jb * JB, (jb + 1) * JB)
        base = jb * 3 * JB
        f1, f2 = lin_ref[0:1, cols], lin_ref[1:2, cols]
        q11, q22, q66 = 2.0 * quad_ref[0:1, cols], 2.0 * quad_ref[1:2, cols], 2.0 * quad_ref[2:3, cols]
        f12 = 2.0 * cross_ref[0:1, cols]
        plies = (ply_ref[0:1, cols] + 1).astype(jnp.float32)
        sums = []
        for at in range(0, cases, tile):
            r = slice(at, at + tile)
            s1 = s_ref[r, base : base + JB]
            s2 = s_ref[r, base + JB : base + 2 * JB]
            t = s_ref[r, base + 2 * JB : base + 3 * JB]
            w = plies * jnp.exp(idx[r, cols] - peak[r])
            w_ref[r, cols] = w
            part = w[:, 0:128]
            for c in range(128, JB, 128):
                part = part + w[:, c : c + 128]
            sums.append(part)
            for k, slope in enumerate((f1 + q11 * s1 + f12 * s2, f2 + q22 * s2 + f12 * s1, q66 * t)):
                value = w * slope
                high = value.astype(jnp.bfloat16)
                at_k = slice(base + k * JB, base + (k + 1) * JB)
                d[r, at_k] = high
                rest[r, at_k] = (value - high.astype(jnp.float32)).astype(jnp.bfloat16)
        total = total + jnp.concatenate(sums, axis=0)
        part = 0.0
        for term in (d, rest):
            part = part + lax.dot_general(
                term[:, base : base + 3 * JB],
                f_ref[:, base : base + 3 * JB],
                (((1,), (1,)), ((), ())),
                preferred_element_type=jnp.float32,
            )
        if jb == 0:
            acc[...] = part
        elif jb < width // JB - 1:
            acc[...] += part
        else:
            total = jnp.sum(total, axis=1, keepdims=True)
            part = (acc[...] + part) * (1.0 / total)
            at = 0
            for ref in term_refs:
                ref[...] = part[at : at + ref.shape[0]].astype(ref.dtype)
                at += ref.shape[0]
    lines = [to_lanes(peak, cases), to_lanes(peak + jnp.log(total), cases)]
    half = cases // 2
    if stat_refs:
        near = stat_refs[0]
        stat_ref[:, 0:half] = near[:, 0:half]
        stat_ref[:, 2 * half : 3 * half] = near[:, half:]
        places = [(half, 0), (3 * half, half)]
    else:
        places = [(0, 0), (half, half)]
    for here, there in places:
        for i in range(2):
            stat_ref[i : i + 1, here : here + half] = lines[i][:, there : there + half]


def join(a, b):
    top = jnp.maximum(a, b)
    return top + jnp.log(jnp.exp(a - top) + jnp.exp(b - top))


def encode(env):
    groups = env.shape[1] // 128
    lines = jnp.concatenate([env[:, g * 128 : (g + 1) * 128] for g in range(groups)], axis=0)
    high = lines.astype(jnp.bfloat16).astype(jnp.float32)
    middle = (lines - high).astype(jnp.bfloat16).astype(jnp.float32)
    rest = jnp.zeros((16 - 3 * groups, 128), jnp.float32)
    return jnp.concatenate([high, middle, lines - high - middle, rest], axis=0).astype(jnp.bfloat16)


def decode(ref, cases):
    size, groups = ref.shape[0] - 16, cases // 128
    lines = ref[size : size + 16, :].astype(jnp.float32)
    lines = lines[0:groups] + lines[groups : 2 * groups] + lines[2 * groups : 3 * groups]
    return jnp.concatenate([lines[g : g + 1] for g in range(groups)], axis=1)


def fold(x):
    return jnp.concatenate([x[:, c : c + 128] for c in range(0, x.shape[1], 128)], axis=0)


def cores_kernel(own_ref, got_ref, stat_ref, twin_ref, out_ref, env_ref):
    quarter = own_ref.shape[0]
    cases = 4 * quarter
    mine, theirs = stat_ref[1:2, :], swap_halves(twin_ref[1:2, :])
    env = join(mine, theirs)
    env_ref[...] = env
    r = slice(quarter, 2 * quarter)
    up = column(jnp.exp(mine - env)[:, r], quarter)
    down = column(jnp.exp(theirs - env)[:, r], quarter)
    value = own_ref[...] * up + got_ref[...] * down
    size = out_ref.shape[0] - 16
    out_ref[0:size, :] = fold(value).astype(jnp.bfloat16)
    out_ref[size : size + 16, :] = encode(env)


def column(row, rows):
    return jnp.concatenate([to_rows(row, at)[:, 0:1] for at in range(0, rows, 128)], axis=0)


def chips_kernel(nz, own_ref, got_ref, stat_ref, twin_ref, part_ref, *refs):
    env_refs, stack_ref, own_out_ref, out_refs = refs[:nz], refs[nz], refs[nz + 1], refs[nz + 2 :]
    quarter = own_ref.shape[0]
    units = own_ref.shape[1]
    cases = 4 * quarter
    rows = quarter // nz
    stack_ref[...] = jnp.concatenate([ref[...] for ref in env_refs], axis=0)
    mine, theirs = stat_ref[1:2, :], swap_halves(twin_ref[1:2, :])
    far = decode(part_ref, cases)
    far = jnp.concatenate([far[:, g * quarter : (g + 1) * quarter] for g in (1, 0, 3, 2)], axis=1)
    env = join(join(mine, theirs), far)
    scale = [column(jnp.exp(x - env)[:, 0:quarter], quarter) for x in (mine, theirs, far)]
    total = own_ref[...] * scale[0] + got_ref[...] * scale[1]
    parts = []
    for c in range(units // 128):
        part = part_ref[c * quarter : (c + 1) * quarter, :].astype(jnp.float32)
        parts.append(total[:, c * 128 : (c + 1) * 128] + part * scale[2])
    own_out_ref[...] = jnp.concatenate([p[0:rows] for p in parts], axis=0)
    for m, ref in enumerate(out_refs):
        r = slice((m + 1) * rows, (m + 2) * rows)
        ref[...] = jnp.concatenate([p[r] for p in parts], axis=0)


def coef_kernel(cot_ref, stat_ref, near_ref, far_ref, s0_ref, s1_ref, w0_ref, w1_ref, coef_ref, gain_ref):
    nz, cases = near_ref.shape
    quarter = cases // 4
    rows = quarter // nz
    width = w0_ref.shape[1]
    row = lax.broadcasted_iota(jnp.int32, (nz, cases), 0)
    near = swap_lanes(near_ref[...], row, rows, 2 * nz)
    far = swap_lanes(far_ref[...], row + nz, rows, 2 * nz)
    env_all = join(near, far)
    top = jnp.max(env_all, axis=0, keepdims=True)
    env = top + jnp.log(jnp.sum(jnp.exp(env_all - top), axis=0, keepdims=True))
    cot = cot_ref[...]
    gain = cot[:, 0:128] * jnp.exp(env_all[:, 0:128] - env[:, 0:128])
    fill = jnp.zeros((128 - nz, 128), jnp.float32)
    gain_ref[...] = jnp.transpose(jnp.concatenate([gain, fill], axis=0))[0:rows]
    scale = cot * jnp.exp(stat_ref[0:1, :] - env)
    scales = [to_rows(scale, at) for at in range(0, cases, 128)]
    sets = [
        (0, s0_ref, w0_ref, 0),
        (quarter, s1_ref, w1_ref, 0),
        (2 * quarter, s0_ref, w0_ref, quarter),
        (3 * quarter, s1_ref, w1_ref, quarter),
    ]
    for jb in range(width // JB):
        base = jb * 3 * JB
        for c in range(0, JB, 128):
            sums = [jnp.zeros((8, 128), jnp.float32) for _ in range(6)]
            for here, s_ref, w_ref, there in sets:
                for at in range(0, quarter, 8):
                    r = slice(there + at, there + at + 8)
                    s1 = s_ref[r, base + c : base + c + 128]
                    s2 = s_ref[r, base + JB + c : base + JB + c + 128]
                    t = s_ref[r, base + 2 * JB + c : base + 2 * JB + c + 128]
                    place = here + at
                    gain = scales[place // 128][place % 128 : place % 128 + 8]
                    w = w_ref[r, jb * JB + c : jb * JB + c + 128] * gain
                    a, b = w * s1, w * s2
                    for i, v in enumerate((a, b, a * s1, b * s2, w * t * t, a * s2)):
                        sums[i] = sums[i] + v
            for i in range(6):
                line = jnp.sum(sums[i], axis=0, keepdims=True)
                if i == 5:
                    line = 2.0 * line
                coef_ref[i : i + 1, jb * JB + c : jb * JB + c + 128] = line


def combine_kernel(gain_ref, own_ref, *refs):
    part_refs, out_ref = refs[-2::-1], refs[-1]
    rows, units = out_ref.shape
    for c in range(units // 128):
        r = slice(c * rows, (c + 1) * rows)
        value = own_ref[r, :] * gain_ref[:, 0:1]
        for m, ref in enumerate(part_refs):
            value = value + ref[r, :] * gain_ref[:, m + 1 : m + 2]
        out_ref[:, c * 128 : (c + 1) * 128] = value


def per_device(n, n_case, load_coef, mantissa, scale_exp, lin_coef, quad_coef, cross_coef, ply_count, cotangent):
    units, comps, width = mantissa.shape
    rows = load_coef.shape[0]
    cases = rows * n
    nz = n // 4
    quarter = rows * nz
    f32, bf16 = jnp.float32, jnp.bfloat16
    shape = jax.ShapeDtypeStruct
    me = lax.axis_index("elem").astype(jnp.int32).reshape(1)

    def along(bits, x):
        return lax.ppermute(x, "elem", [(i, i ^ bits) for i in range(n)])

    along_z = [along(4 * m, load_coef) for m in range(nz - 1, 0, -1)]
    fields, cot = vmem_call(
        functools.partial(prep_kernel, n),
        [shape((units, comps * width), bf16), shape((1, cases), f32)],
        scratch_shapes=[
            VMEM((comps, units, width), bf16),
            VMEM((comps, scale_exp.shape[2], units), jnp.int32),
            VMEM((1, cases), f32),
            pltpu.SemaphoreType.DMA((comps + 2,)),
        ],
        flops=units * comps * width,
        nbytes=4 * units * comps * width,
        n_in=4,
        smem=(0,),
        hbm=(1, 2, 3),
    )(
        me,
        pltpu.with_memory_space_constraint(jnp.transpose(mantissa, (1, 0, 2)), pltpu.HBM),
        pltpu.with_memory_space_constraint(jnp.transpose(scale_exp, (1, 2, 0)), pltpu.HBM),
        pltpu.with_memory_space_constraint(cotangent.reshape(1, cases), pltpu.HBM),
    )
    along_z[0], fields = lax.optimization_barrier((along_z[0], fields))
    near = vmem_call(block_kernel, shape((quarter, units), bf16), nbytes=4 * quarter * units, n_in=nz)(
        *along_z, load_coef
    )
    far = along(2, near)
    near_twin = along(1, near)

    def main(blocks, dtypes, stats=()):
        count = len(blocks) * quarter
        outs = vmem_call(
            functools.partial(main_kernel, len(blocks), len(stats)),
            [shape((quarter, units), dtype) for dtype in dtypes]
            + [
                shape((2, cases if stats else count), f32),
                shape((count, comps * width), f32),
                shape((count, width), f32),
            ],
            scratch_shapes=[
                VMEM((count, units), bf16),
                VMEM((count, width), f32),
                VMEM((count, comps * width), bf16),
                VMEM((count, comps * width), bf16),
                VMEM((count, units), f32),
            ],
            flops=6 * count * units * comps * width,
            nbytes=2 * units * comps * width + 4 * count * 4 * width,
            exps=count * width,
            n_in=5 + len(blocks) + len(stats),
            limit=24,
        )(
            fields,
            lin_coef,
            quad_coef,
            cross_coef.reshape(1, width),
            ply_count.reshape(1, width),
            *blocks,
            *stats,
        )
        return outs

    near_own, near_send, near_stat, s0, w0 = main([near, near_twin], [f32, f32])
    far, near_send = lax.optimization_barrier((far, near_send))
    far_own, far_send, stat, s1, w1 = main([far, along(1, far)], [f32, f32], [near_stat])
    far_got, stat_twin = along(1, far_send), along(1, stat)

    chunk, env = vmem_call(
        cores_kernel,
        [shape((quarter * units // 128 + 16, 128), bf16), shape((1, cases), f32)],
        flops=4 * quarter * units,
        nbytes=8 * quarter * units,
        n_in=4,
    )(far_own, far_got, stat, stat_twin)
    chunk, near_send = lax.optimization_barrier((chunk, near_send))
    part, near_got = along(2, chunk), along(1, near_send)
    envs = [along(4 * m, env) for m in range(nz - 1, 0, -1)]
    outs = vmem_call(
        functools.partial(chips_kernel, nz),
        [shape((nz, cases), f32), shape((rows * units // 128, 128), f32)]
        + [shape((rows * units // 128, 128), f32)] * (nz - 1),
        flops=6 * quarter * units,
        nbytes=10 * quarter * units,
        n_in=5 + nz,
    )(near_own, near_got, stat, stat_twin, part, env, *envs[::-1])
    stack, own = outs[:2]
    stack_far = along(2, stack)
    parts = [along(4 * m, outs[1 + m]) for m in range(nz - 1, 0, -1)]

    coef, gain = vmem_call(
        coef_kernel,
        [shape((6, width), f32), shape((rows, 128), f32)],
        flops=14 * cases * width,
        nbytes=16 * cases * width,
        n_in=8,
    )(cot, stat, stack, stack_far, s0, s1, w0, w1)
    bit = 1
    while bit < n_case:
        coef = coef + lax.ppermute(coef, "case", [(i, i ^ bit) for i in range(n_case)])
        bit *= 2

    load_grad = vmem_call(
        combine_kernel,
        shape((rows, units), f32),
        flops=2 * nz * rows * units,
        nbytes=2 * nz * rows * units,
        n_in=2 + len(parts),
    )(gain, own, *parts)
    return (load_grad, coef)


def solution(mesh):
    n, n_case = mesh.shape["elem"], mesh.shape["case"]
    return jax.shard_map(
        functools.partial(per_device, n, n_case),
        mesh=mesh,
        in_specs=(
            P(("case", "elem"), None),
            P(None, None, "elem"),
            P(None, None, "elem"),
            P(None, "elem"),
            P(None, "elem"),
            P("elem"),
            P("elem"),
            P("case"),
        ),
        out_specs=(P(("case", "elem"), None), P(None, "elem")),
        check_vma=False,
    )
```

```python
import functools

import jax
import jax.numpy as jnp
from jax import lax
from jax.experimental import pallas as pl
from jax.experimental.pallas import tpu as pltpu
from jax.sharding import PartitionSpec as P

JB = 256
VMEM = pltpu.VMEM


def vmem_call(kernel, out_shape, scratch_shapes=(), flops=0, nbytes=0, exps=0, n_in=0, smem=(), hbm=(), limit=16):
    def place(i):
        return pltpu.SMEM if i in smem else pltpu.HBM if i in hbm else VMEM

    return pl.pallas_call(
        kernel,
        out_shape=out_shape,
        in_specs=[pl.BlockSpec(memory_space=place(i)) for i in range(n_in)],
        out_specs=jax.tree.map(lambda _: pl.BlockSpec(memory_space=VMEM), out_shape),
        scratch_shapes=list(scratch_shapes),
        cost_estimate=pl.CostEstimate(flops=flops, bytes_accessed=nbytes, transcendentals=exps),
        compiler_params=pltpu.CompilerParams(vmem_limit_bytes=limit << 20),
    )


def to_lanes(column, rows):
    step = min(rows, 128)
    parts = []
    for at in range(0, rows, step):
        square = jnp.broadcast_to(column[at : at + step], (step, 128))
        parts.append(jnp.transpose(square)[0:1, :])
    return jnp.concatenate(parts, axis=1)


def to_rows(row, at):
    return jnp.transpose(jnp.broadcast_to(row[:, at : at + 128], (128, 128)))


def swap_lanes(x, which, width, n):
    lane = lax.broadcasted_iota(jnp.int32, x.shape, 1)
    bit = 1
    while bit < n:
        step = bit * width
        ahead = jnp.concatenate([x[:, step:], x[:, :step]], axis=1)
        behind = jnp.concatenate([x[:, -step:], x[:, :-step]], axis=1)
        other = jnp.where((lane & step) != 0, behind, ahead)
        x = jnp.where((which & bit) != 0, other, x)
        bit *= 2
    return x


def swap_halves(x):
    half = x.shape[1] // 2
    return jnp.concatenate([x[:, half:], x[:, :half]], axis=1)


def block_kernel(*refs):
    out_ref = refs[-1]
    values = [ref[...].astype(jnp.float32) for ref in refs[-2::-1]]
    out_ref[...] = jnp.concatenate(values, axis=0).astype(jnp.bfloat16)


def prep_kernel(n, me_ref, mant_hbm, exp_hbm, cot_hbm, out_ref, cot_out_ref, mant, expo, cot_ref, sems):
    comps, units, width = mant.shape
    blocks = expo.shape[1]
    span = width // blocks
    copies = [
        pltpu.make_async_copy(cot_hbm, cot_ref, sems.at[comps + 1]),
        pltpu.make_async_copy(exp_hbm, expo, sems.at[comps]),
    ]
    copies += [pltpu.make_async_copy(mant_hbm.at[k], mant.at[k], sems.at[k]) for k in range(comps)]
    for copy in copies:
        copy.start()
    copies[0].wait()
    cases = cot_ref.shape[1]
    rows = cases // n
    nz = n // 4
    order = [z * 4 + y * 2 + c for c in range(2) for y in range(2) for z in range(nz)]
    cot = jnp.concatenate([cot_ref[:, e * rows : (e + 1) * rows] for e in order], axis=1)
    code = (me_ref[0] & 1) * (2 * nz) + ((me_ref[0] >> 1) & 1) * nz + (me_ref[0] >> 2)
    cot = jnp.broadcast_to(cot, (8, cases))
    cot_out_ref[...] = swap_lanes(cot, jnp.full((8, cases), code, jnp.int32), rows, n)[0:1]
    copies[1].wait()
    factor = jnp.exp2(expo[...].astype(jnp.float32)).reshape(comps * blocks, units)
    pad = jnp.zeros((128 - comps * blocks, units), jnp.float32)
    columns = jnp.transpose(jnp.concatenate([factor, pad], axis=0))
    for k in range(comps):
        copies[2 + k].wait()
        for b in range(blocks):
            gain = jnp.broadcast_to(columns[:, k * blocks + b : k * blocks + b + 1], (units, span))
            value = mant[k, :, b * span : (b + 1) * span] * gain.astype(jnp.bfloat16)
            first = b * span
            at = (first // JB) * (comps * JB) + k * JB + first % JB
            out_ref[:, at : at + span] = value


def main_kernel(n_rows, n_stat, f_ref, lin_ref, quad_ref, cross_ref, ply_ref, *refs):
    row_refs, stat_refs = refs[:n_rows], refs[n_rows : n_rows + n_stat]
    term_refs = refs[n_rows + n_stat : 2 * n_rows + n_stat]
    stat_ref, s_ref, w_ref, a_ref, idx, d, rest, acc = refs[2 * n_rows + n_stat :]
    cases = a_ref.shape[0]
    width = w_ref.shape[1]
    at = 0
    for ref in row_refs:
        a_ref[at : at + ref.shape[0], :] = ref[...]
        at += ref.shape[0]
    tile = 32
    peak = jnp.full((cases, 128), -jnp.inf, jnp.float32)
    for jb in range(width // JB):
        cols = slice(jb * JB, (jb + 1) * JB)
        base = jb * 3 * JB
        s_ref[:, base : base + 3 * JB] = jnp.dot(
            a_ref[...], f_ref[:, base : base + 3 * JB], preferred_element_type=jnp.float32
        )
        f1, f2 = lin_ref[0:1, cols], lin_ref[1:2, cols]
        f11, f22, f66 = quad_ref[0:1, cols], quad_ref[1:2, cols], quad_ref[2:3, cols]
        f12 = 2.0 * cross_ref[0:1, cols]
        tops = []
        for at in range(0, cases, tile):
            r = slice(at, at + tile)
            s1 = s_ref[r, base : base + JB]
            s2 = s_ref[r, base + JB : base + 2 * JB]
            t = s_ref[r, base + 2 * JB : base + 3 * JB]
            index = s1 * (f1 + f11 * s1 + f12 * s2) + s2 * (f2 + f22 * s2) + f66 * (t * t)
            idx[r, cols] = index
            top = index[:, 0:128]
            for c in range(128, JB, 128):
                top = jnp.maximum(top, index[:, c : c + 128])
            tops.append(top)
        peak = jnp.maximum(peak, jnp.concatenate(tops, axis=0))
    peak = jnp.max(peak, axis=1, keepdims=True)

    total = jnp.zeros((cases, 128), jnp.float32)
    for jb in range(width // JB):
        cols = slice(jb * JB, (jb + 1) * JB)
        base = jb * 3 * JB
        f1, f2 = lin_ref[0:1, cols], lin_ref[1:2, cols]
        q11, q22, q66 = 2.0 * quad_ref[0:1, cols], 2.0 * quad_ref[1:2, cols], 2.0 * quad_ref[2:3, cols]
        f12 = 2.0 * cross_ref[0:1, cols]
        plies = (ply_ref[0:1, cols] + 1).astype(jnp.float32)
        sums = []
        for at in range(0, cases, tile):
            r = slice(at, at + tile)
            s1 = s_ref[r, base : base + JB]
            s2 = s_ref[r, base + JB : base + 2 * JB]
            t = s_ref[r, base + 2 * JB : base + 3 * JB]
            w = plies * jnp.exp(idx[r, cols] - peak[r])
            w_ref[r, cols] = w
            part = w[:, 0:128]
            for c in range(128, JB, 128):
                part = part + w[:, c : c + 128]
            sums.append(part)
            for k, slope in enumerate((f1 + q11 * s1 + f12 * s2, f2 + q22 * s2 + f12 * s1, q66 * t)):
                value = w * slope
                high = value.astype(jnp.bfloat16)
                at_k = slice(base + k * JB, base + (k + 1) * JB)
                d[r, at_k] = high
                rest[r, at_k] = (value - high.astype(jnp.float32)).astype(jnp.bfloat16)
        total = total + jnp.concatenate(sums, axis=0)
        part = 0.0
        for term in (d, rest):
            part = part + lax.dot_general(
                term[:, base : base + 3 * JB],
                f_ref[:, base : base + 3 * JB],
                (((1,), (1,)), ((), ())),
                preferred_element_type=jnp.float32,
            )
        if jb == 0:
            acc[...] = part
        elif jb < width // JB - 1:
            acc[...] += part
        else:
            total = jnp.sum(total, axis=1, keepdims=True)
            part = (acc[...] + part) * (1.0 / total)
            at = 0
            for ref in term_refs:
                ref[...] = part[at : at + ref.shape[0]].astype(ref.dtype)
                at += ref.shape[0]
    lines = [to_lanes(peak, cases), to_lanes(peak + jnp.log(total), cases)]
    half = cases // 2
    if stat_refs:
        near = stat_refs[0]
        stat_ref[:, 0:half] = near[:, 0:half]
        stat_ref[:, 2 * half : 3 * half] = near[:, half:]
        places = [(half, 0), (3 * half, half)]
    else:
        places = [(0, 0), (half, half)]
    for here, there in places:
        for i in range(2):
            stat_ref[i : i + 1, here : here + half] = lines[i][:, there : there + half]


def join(a, b):
    top = jnp.maximum(a, b)
    return top + jnp.log(jnp.exp(a - top) + jnp.exp(b - top))


def encode(env):
    groups = env.shape[1] // 128
    lines = jnp.concatenate([env[:, g * 128 : (g + 1) * 128] for g in range(groups)], axis=0)
    high = lines.astype(jnp.bfloat16).astype(jnp.float32)
    middle = (lines - high).astype(jnp.bfloat16).astype(jnp.float32)
    rest = jnp.zeros((16 - 3 * groups, 128), jnp.float32)
    return jnp.concatenate([high, middle, lines - high - middle, rest], axis=0).astype(jnp.bfloat16)


def decode(ref, cases):
    size, groups = ref.shape[0] - 16, cases // 128
    lines = ref[size : size + 16, :].astype(jnp.float32)
    lines = lines[0:groups] + lines[groups : 2 * groups] + lines[2 * groups : 3 * groups]
    return jnp.concatenate([lines[g : g + 1] for g in range(groups)], axis=1)


def fold(x):
    return jnp.concatenate([x[:, c : c + 128] for c in range(0, x.shape[1], 128)], axis=0)


def cores_kernel(own_ref, got_ref, stat_ref, twin_ref, out_ref, env_ref):
    quarter = own_ref.shape[0]
    cases = 4 * quarter
    mine, theirs = stat_ref[1:2, :], swap_halves(twin_ref[1:2, :])
    env = join(mine, theirs)
    env_ref[...] = env
    r = slice(quarter, 2 * quarter)
    up = column(jnp.exp(mine - env)[:, r], quarter)
    down = column(jnp.exp(theirs - env)[:, r], quarter)
    value = own_ref[...] * up + got_ref[...] * down
    size = out_ref.shape[0] - 16
    out_ref[0:size, :] = fold(value).astype(jnp.bfloat16)
    out_ref[size : size + 16, :] = encode(env)


def column(row, rows):
    return jnp.concatenate([to_rows(row, at)[:, 0:1] for at in range(0, rows, 128)], axis=0)


def chips_kernel(nz, own_ref, got_ref, stat_ref, twin_ref, part_ref, *refs):
    env_refs, stack_ref, own_out_ref, out_refs = refs[:nz], refs[nz], refs[nz + 1], refs[nz + 2 :]
    quarter = own_ref.shape[0]
    units = own_ref.shape[1]
    cases = 4 * quarter
    rows = quarter // nz
    stack_ref[...] = jnp.concatenate([ref[...] for ref in env_refs], axis=0)
    mine, theirs = stat_ref[1:2, :], swap_halves(twin_ref[1:2, :])
    far = decode(part_ref, cases)
    far = jnp.concatenate([far[:, g * quarter : (g + 1) * quarter] for g in (1, 0, 3, 2)], axis=1)
    env = join(join(mine, theirs), far)
    scale = [column(jnp.exp(x - env)[:, 0:quarter], quarter) for x in (mine, theirs, far)]
    total = own_ref[...] * scale[0] + got_ref[...] * scale[1]
    parts = []
    for c in range(units // 128):
        part = part_ref[c * quarter : (c + 1) * quarter, :].astype(jnp.float32)
        parts.append(total[:, c * 128 : (c + 1) * 128] + part * scale[2])
    own_out_ref[...] = jnp.concatenate([p[0:rows] for p in parts], axis=0)
    for m, ref in enumerate(out_refs):
        r = slice((m + 1) * rows, (m + 2) * rows)
        ref[...] = jnp.concatenate([p[r] for p in parts], axis=0).astype(jnp.bfloat16)


def coef_kernel(cot_ref, stat_ref, near_ref, far_ref, s0_ref, s1_ref, w0_ref, w1_ref, coef_ref, gain_ref):
    nz, cases = near_ref.shape
    quarter = cases // 4
    rows = quarter // nz
    width = w0_ref.shape[1]
    row = lax.broadcasted_iota(jnp.int32, (nz, cases), 0)
    near = swap_lanes(near_ref[...], row, rows, 2 * nz)
    far = swap_lanes(far_ref[...], row + nz, rows, 2 * nz)
    env_all = join(near, far)
    top = jnp.max(env_all, axis=0, keepdims=True)
    env = top + jnp.log(jnp.sum(jnp.exp(env_all - top), axis=0, keepdims=True))
    cot = cot_ref[...]
    gain = cot[:, 0:128] * jnp.exp(env_all[:, 0:128] - env[:, 0:128])
    fill = jnp.zeros((128 - nz, 128), jnp.float32)
    gain_ref[...] = jnp.transpose(jnp.concatenate([gain, fill], axis=0))[0:rows]
    scale = cot * jnp.exp(stat_ref[0:1, :] - env)
    scales = [to_rows(scale, at) for at in range(0, cases, 128)]
    sets = [
        (0, s0_ref, w0_ref, 0),
        (quarter, s1_ref, w1_ref, 0),
        (2 * quarter, s0_ref, w0_ref, quarter),
        (3 * quarter, s1_ref, w1_ref, quarter),
    ]
    for jb in range(width // JB):
        base = jb * 3 * JB
        for c in range(0, JB, 128):
            sums = [jnp.zeros((8, 128), jnp.float32) for _ in range(6)]
            for here, s_ref, w_ref, there in sets:
                for at in range(0, quarter, 8):
                    r = slice(there + at, there + at + 8)
                    s1 = s_ref[r, base + c : base + c + 128]
                    s2 = s_ref[r, base + JB + c : base + JB + c + 128]
                    t = s_ref[r, base + 2 * JB + c : base + 2 * JB + c + 128]
                    place = here + at
                    gain = scales[place // 128][place % 128 : place % 128 + 8]
                    w = w_ref[r, jb * JB + c : jb * JB + c + 128] * gain
                    a, b = w * s1, w * s2
                    for i, v in enumerate((a, b, a * s1, b * s2, w * t * t, a * s2)):
                        sums[i] = sums[i] + v
            for i in range(6):
                line = jnp.sum(sums[i], axis=0, keepdims=True)
                if i == 5:
                    line = 2.0 * line
                coef_ref[i : i + 1, jb * JB + c : jb * JB + c + 128] = line


def combine_kernel(gain_ref, own_ref, *refs):
    part_refs, out_ref = refs[-2::-1], refs[-1]
    rows, units = out_ref.shape
    for c in range(units // 128):
        r = slice(c * rows, (c + 1) * rows)
        value = own_ref[r, :] * gain_ref[:, 0:1]
        for m, ref in enumerate(part_refs):
            part = ref[...].astype(jnp.float32)[r]
            value = value + part * gain_ref[:, m + 1 : m + 2]
        out_ref[:, c * 128 : (c + 1) * 128] = value


def per_device(n, n_case, load_coef, mantissa, scale_exp, lin_coef, quad_coef, cross_coef, ply_count, cotangent):
    units, comps, width = mantissa.shape
    rows = load_coef.shape[0]
    cases = rows * n
    nz = n // 4
    quarter = rows * nz
    f32, bf16 = jnp.float32, jnp.bfloat16
    shape = jax.ShapeDtypeStruct
    me = lax.axis_index("elem").astype(jnp.int32).reshape(1)

    def along(bits, x):
        return lax.ppermute(x, "elem", [(i, i ^ bits) for i in range(n)])

    along_z = [along(4 * m, load_coef) for m in range(nz - 1, 0, -1)]
    fields, cot = vmem_call(
        functools.partial(prep_kernel, n),
        [shape((units, comps * width), bf16), shape((1, cases), f32)],
        scratch_shapes=[
            VMEM((comps, units, width), bf16),
            VMEM((comps, scale_exp.shape[2], units), jnp.int32),
            VMEM((1, cases), f32),
            pltpu.SemaphoreType.DMA((comps + 2,)),
        ],
        flops=units * comps * width,
        nbytes=4 * units * comps * width,
        n_in=4,
        smem=(0,),
        hbm=(1, 2, 3),
    )(
        me,
        pltpu.with_memory_space_constraint(jnp.transpose(mantissa, (1, 0, 2)), pltpu.HBM),
        pltpu.with_memory_space_constraint(jnp.transpose(scale_exp, (1, 2, 0)), pltpu.HBM),
        pltpu.with_memory_space_constraint(cotangent.reshape(1, cases), pltpu.HBM),
    )
    along_z[0], fields = lax.optimization_barrier((along_z[0], fields))
    near = vmem_call(block_kernel, shape((quarter, units), bf16), nbytes=4 * quarter * units, n_in=nz)(
        *along_z, load_coef
    )
    far = along(2, near)
    near_twin = along(1, near)

    def main(blocks, dtypes, stats=()):
        count = len(blocks) * quarter
        outs = vmem_call(
            functools.partial(main_kernel, len(blocks), len(stats)),
            [shape((quarter, units), dtype) for dtype in dtypes]
            + [
                shape((2, cases if stats else count), f32),
                shape((count, comps * width), f32),
                shape((count, width), f32),
            ],
            scratch_shapes=[
                VMEM((count, units), bf16),
                VMEM((count, width), f32),
                VMEM((count, comps * width), bf16),
                VMEM((count, comps * width), bf16),
                VMEM((count, units), f32),
            ],
            flops=6 * count * units * comps * width,
            nbytes=2 * units * comps * width + 4 * count * 4 * width,
            exps=count * width,
            n_in=5 + len(blocks) + len(stats),
            limit=24,
        )(
            fields,
            lin_coef,
            quad_coef,
            cross_coef.reshape(1, width),
            ply_count.reshape(1, width),
            *blocks,
            *stats,
        )
        return outs

    near_own, near_send, near_stat, s0, w0 = main([near, near_twin], [f32, f32])
    far, near_send = lax.optimization_barrier((far, near_send))
    far_own, far_send, stat, s1, w1 = main([far, along(1, far)], [f32, f32], [near_stat])
    far_got, stat_twin = along(1, far_send), along(1, stat)

    chunk, env = vmem_call(
        cores_kernel,
        [shape((quarter * units // 128 + 16, 128), bf16), shape((1, cases), f32)],
        flops=4 * quarter * units,
        nbytes=8 * quarter * units,
        n_in=4,
    )(far_own, far_got, stat, stat_twin)
    chunk, near_send = lax.optimization_barrier((chunk, near_send))
    part, near_got = along(2, chunk), along(1, near_send)
    envs = [along(4 * m, env) for m in range(nz - 1, 0, -1)]
    outs = vmem_call(
        functools.partial(chips_kernel, nz),
        [shape((nz, cases), f32), shape((rows * units // 128, 128), f32)]
        + [shape((rows * units // 128, 128), bf16)] * (nz - 1),
        flops=6 * quarter * units,
        nbytes=10 * quarter * units,
        n_in=5 + nz,
    )(near_own, near_got, stat, stat_twin, part, env, *envs[::-1])
    stack, own = outs[:2]
    stack_far = along(2, stack)
    parts = [along(4 * m, outs[1 + m]) for m in range(nz - 1, 0, -1)]

    coef, gain = vmem_call(
        coef_kernel,
        [shape((6, width), f32), shape((rows, 128), f32)],
        flops=14 * cases * width,
        nbytes=16 * cases * width,
        n_in=8,
    )(cot, stat, stack, stack_far, s0, s1, w0, w1)
    load_grad = vmem_call(
        combine_kernel,
        shape((rows, units), f32),
        flops=2 * nz * rows * units,
        nbytes=2 * nz * rows * units,
        n_in=2 + len(parts),
    )(gain, own, *parts)
    bit = 1
    while bit < n_case:
        got = lax.ppermute(coef, "case", [(i, i ^ bit) for i in range(n_case)])
        load_grad, got = lax.optimization_barrier((load_grad, got))
        coef = coef + got
        bit *= 2
    return (load_grad, coef)


def solution(mesh):
    n, n_case = mesh.shape["elem"], mesh.shape["case"]
    return jax.shard_map(
        functools.partial(per_device, n, n_case),
        mesh=mesh,
        in_specs=(
            P(("case", "elem"), None),
            P(None, None, "elem"),
            P(None, None, "elem"),
            P(None, "elem"),
            P(None, "elem"),
            P("elem"),
            P("elem"),
            P("case"),
        ),
        out_specs=(P(("case", "elem"), None), P(None, "elem")),
        check_vma=False,
    )
```
